1024 devices in a mesh: feat: 64 (over z, core), dp: 16 (over x, y).
Axes of the slice: x: 4, y: 4, z: 32, core: 2. Of those that a mesh axis runs over, the one named last changes fastest.
Arguments:
- features: bfloat16 [16, 1024, 2048], P('dp', 'feat'), may hold values from -6 to 6
- neigh_lists: int32 [16, 10, 1024], P('dp'), may hold values from 0 to 2047
- w1_self: bfloat16 [1024, 512], P('feat'), may hold values from -0.125 to 0.125
- w1_neigh: bfloat16 [1024, 512], P('feat'), may hold values from -0.125 to 0.125
- w2_self: bfloat16 [512, 512], replicated, may hold values from -0.1875 to 0.1875
- w2_neigh: bfloat16 [512, 512], replicated, may hold values from -0.1875 to 0.1875
- send_rows: int32 [16, 64, 16, 8], P('dp', 'feat'), may hold values from 0 to 15
- send_count: int32 [16, 64, 16], P('dp', 'feat'), may hold values from 1 to 8, as said below
- recv_target: int32 [16, 64, 16, 8], P('dp', 'feat'), may hold values from 0 to 15
- out_grad: bfloat16 [16, 64, 16, 512], P('dp', 'feat'), may hold values from -6 to 6
Outputs:
- layer_out: bfloat16 [16, 64, 16, 512], P('dp', 'feat')
- grad_w1_self: float32 [16, 1024, 512], P('dp', 'feat')
- grad_w1_neigh: float32 [16, 1024, 512], P('dp', 'feat')
The draws below stay inside these ranges and needn't reach their ends.
Inputs may be any that keep to these rules, and one draw needn't show every extreme that they name: `send_count`: for each feat index one data index, drawn from the seed, receives 8 live slots from every data peer; every other count is at most 4. `recv_target`: slots at or beyond the sending device's count carry nothing.
All inputs are finite; a program needn't handle non-finite values.
Results may differ from the reference program's by a relative error of at most 0.0277.
Values may be sent and summed in bfloat16 or wider, within the bound.
A program may use at most 32 MiB of HBM per device.

```python
import jax
import jax.numpy as jnp
from jax import lax

D = 1024
H = 512
H2 = 512
ROW_DEV = 16
K1 = 10
CAP = 8
S = 1024
SX = 2048
N_FEAT = 64
N_DP = 16


def draw_send_count(key, part):
    key = jax.random.fold_in(key, 11)
    base_key, hot_key = jax.random.split(key)
    base = jax.random.randint(base_key, (N_DP, N_FEAT, N_DP), 1, CAP // 2 + 1)
    hottest = jax.random.randint(hot_key, (N_FEAT,), 0, N_DP)
    is_hot = jnp.arange(N_DP, dtype=jnp.int32)[None, :] == hottest[:, None]
    return jnp.where(is_hot[None, :, :], CAP, base).astype(jnp.int32)


def plant(values, own_key, low, largest):
    place = [jax.random.randint(jax.random.fold_in(own_key, axis), (), 0, length) for axis, length in enumerate(values.shape)]
    main_axis = values.shape.index(max(values.shape))
    next_to = place[:main_axis] + [(place[main_axis] + 1) % values.shape[main_axis]] + place[main_axis + 1:]
    return values.at[tuple(place)].set(low).at[tuple(next_to)].set(largest)


def level_of(key, extent, shards, smallest, high):
    gain = 1.0
    for axis_at, blocks in shards:
        draws = jax.random.uniform(jax.random.fold_in(jax.random.fold_in(key, 6), axis_at), (blocks,), jnp.float32, smallest / len(shards), high / len(shards))
        gain = gain * jnp.repeat(jnp.exp(draws), extent[axis_at] // blocks).reshape((-1,) + (1,) * (len(extent) - 1 - axis_at))
    return gain


def noise(stream_key, dims, width, reach, shards=(), kind=jnp.bfloat16):
    factor_of = level_of(stream_key, dims, shards, -0.22, 0.18) if shards else 1.0
    array = jax.random.normal(stream_key, dims, jnp.float32) * width * factor_of
    return jnp.minimum(jnp.maximum(array, -reach), reach).astype(kind)


def setup_inputs(seed: int = 0) -> dict:
    keys = jax.random.split(jax.random.key(seed), 11)
    return {
        "features": noise(keys[0], (N_DP, D, SX), 1.0, 6.0, ((0, 16), (1, 64))),
        "neigh_lists": plant(jax.random.randint(keys[1], (N_DP, K1, S), 0, SX), jax.random.fold_in(keys[1], 1), 0, SX - 1).astype(jnp.int32),
        "w1_self": noise(keys[2], (D, H), (2 * D) ** -0.5, 0.125, ((0, 64),)),
        "w1_neigh": noise(keys[3], (D, H), (2 * D) ** -0.5, 0.125, ((0, 64),)),
        "w2_self": noise(keys[4], (H, H2), (2 * H) ** -0.5, 0.1875),
        "w2_neigh": noise(keys[5], (H, H2), (2 * H) ** -0.5, 0.1875),
        "send_rows": plant(jax.random.randint(keys[6], (N_DP, N_FEAT, N_DP, CAP), 0, ROW_DEV), jax.random.fold_in(keys[6], 1), 0, ROW_DEV - 1).astype(jnp.int32),
        "send_count": draw_send_count(jax.random.fold_in(keys[10], 71), 0),
        "recv_target": plant(jax.random.randint(keys[8], (N_DP, N_FEAT, N_DP, CAP), 0, ROW_DEV), jax.random.fold_in(keys[8], 1), 0, ROW_DEV - 1).astype(jnp.int32),
        "out_grad": noise(keys[9], (N_DP, N_FEAT, ROW_DEV, H2), 1.0, 6.0, ((0, 16), (1, 64))),
    }


def first_layer(columns, neighbour_lists, w1_self, w1_neigh):
    self_cols = columns[:, :S]
    gathered = jnp.take(columns, neighbour_lists, axis=1)
    mean_cols = (jnp.sum(gathered.astype(jnp.float32), axis=1) / K1).astype(jnp.bfloat16)
    contract = (((0,), (0,)), ((), ()))
    preact = lax.dot_general(self_cols, w1_self, contract, preferred_element_type=jnp.float32)
    preact = preact + lax.dot_general(mean_cols, w1_neigh, contract, preferred_element_type=jnp.float32)
    return self_cols, mean_cols, preact


def add_rows(indices, values):
    zeroed = jnp.zeros((ROW_DEV, values.shape[-1]), jnp.float32)
    return zeroed.at[indices.reshape(-1)].add(values.reshape(-1, values.shape[-1]))


def reference(features, neigh_lists, w1_self, w1_neigh, w2_self, w2_neigh, send_rows, send_count, recv_target, out_grad):
    def group_step(inputs):
        return first_layer(inputs[0], inputs[1], w1_self, w1_neigh)

    self_all, mean_all, pre_all = lax.map(group_step, (features, neigh_lists))
    hidden = jnp.maximum(pre_all, 0.0).astype(jnp.bfloat16).reshape(N_DP, N_FEAT, ROW_DEV, H)
    transposed = (((1,), (1,)), ((), ()))

    def per_device(hidden_rows, contrib, targets, usable, upstream):
        neigh_sum = add_rows(targets, contrib)
        degree = jnp.zeros((ROW_DEV,), jnp.float32).at[targets.reshape(-1)].add(usable.reshape(-1).astype(jnp.float32))[:, None]
        mean_two = ((hidden_rows.astype(jnp.float32) + neigh_sum) / (1.0 + degree)).astype(jnp.bfloat16)
        output = jnp.dot(hidden_rows, w2_self, preferred_element_type=jnp.float32)
        output = (output + jnp.dot(mean_two, w2_neigh, preferred_element_type=jnp.float32)).astype(jnp.bfloat16)
        grad_self = lax.dot_general(upstream, w2_self, transposed, preferred_element_type=jnp.float32)
        grad_mean = lax.dot_general(upstream, w2_neigh, transposed, preferred_element_type=jnp.float32) / (1.0 + degree)
        returning = jnp.where(usable[..., None], jnp.take(grad_mean, targets, axis=0), 0.0)
        return output, grad_self + grad_mean, returning

    def second_layer(inputs):
        rows_feat, sends, counts, targets, upstream = inputs
        outgoing = jax.vmap(jnp.take, in_axes=(0, 0, None))(rows_feat, sends, 0)
        incoming = jnp.swapaxes(outgoing, 0, 1)
        slot_ids = jnp.arange(CAP, dtype=jnp.int32)
        usable = slot_ids[None, None, :] < jnp.swapaxes(counts, 0, 1)[:, :, None]
        contrib = jnp.where(usable[..., None], incoming.astype(jnp.float32), 0.0)
        outputs, grad_local, returning = jax.vmap(per_device)(rows_feat, contrib, targets, usable, upstream)
        arrived = jnp.swapaxes(returning, 0, 1)
        back_sum = jax.vmap(add_rows)(sends, arrived)
        return outputs, grad_local + back_sum

    outputs, grad_hidden = lax.map(second_layer, (jnp.swapaxes(hidden, 0, 1), jnp.swapaxes(send_rows, 0, 1), jnp.swapaxes(send_count, 0, 1), jnp.swapaxes(recv_target, 0, 1), jnp.swapaxes(out_grad, 0, 1)))
    layer_out = jnp.swapaxes(outputs, 0, 1)
    grad_hidden = jnp.swapaxes(grad_hidden, 0, 1).reshape(N_DP, S, H)
    grad_pre = jnp.where(pre_all > 0, grad_hidden, 0.0).astype(jnp.bfloat16)

    def weight_grads(inputs):
        self_cols, mean_cols, grad_rows = inputs
        return (jnp.dot(self_cols, grad_rows, preferred_element_type=jnp.float32), jnp.dot(mean_cols, grad_rows, preferred_element_type=jnp.float32))

    grad_w1_self, grad_w1_neigh = lax.map(weight_grads, (self_all, mean_all, grad_pre))
    return layer_out, grad_w1_self, grad_w1_neigh
```

```python
import jax
import jax.numpy as jnp
from jax import lax
from jax.experimental import pallas as pl
from jax.experimental.pallas import tpu as pltpu
from jax.sharding import PartitionSpec as P

MESH = pl.DeviceIdType.MESH
K1 = 10
NZ = 32
NDP = 16
GROUPS = 8
LANES = 128
F32 = jnp.float32
BF16 = jnp.bfloat16

AG_PLAN = (
    (0, (8, -8, 4, -4, 1, -1, 2, -2)),
    (-4, (1, -1, 2)),
    (4, (1, -1, -2)),
    (-8, (8, 4, 1, -1, 2)),
    (8, (-4, 1, -1, -2)),
    (-12, (1, -1, 2)),
    (12, (1, -1, -2)),
    (16, (1, -1)),
)


def iota(shape, axis):
    return lax.broadcasted_iota(jnp.int32, shape, axis)


def dot(a, b):
    return jnp.dot(a, b, preferred_element_type=F32)


def dot_nt(a, b):
    return lax.dot_general(a, b, (((1,), (1,)), ((), ())), preferred_element_type=F32)


def kernel(
    feat_ref,
    lists_ref,
    w1s_ref,
    w1n_ref,
    w2s_ref,
    w2n_ref,
    rows_ref,
    count_ref,
    target_ref,
    og_ref,
    out_ref,
    gs_ref,
    gn_ref,
    xs,
    xp,
    xf,
    xt,
    xn,
    w,
    meta,
    gm_all,
    h_all,
    gp,
    part,
    part_in,
    res,
    res_in,
    w1f_s,
    w1f_r,
    far_s,
    far_r,
    near_s,
    near_r,
    wd_s,
    wd_r,
    meta_s,
    meta_r,
    gm_s,
    gm_r,
    h_s,
    h_r,
    ag_s,
    ag_r,
    d2d_s,
    d2d_r,
):
    f = lax.axis_index("feat")
    d = lax.axis_index("dp")
    z = f // 2
    q = lax.rem(f, 2)
    g = z // 4
    zeta = lax.rem(z, 4)
    partner = 2 * z + 1 - q

    def chip(zz):
        return {"feat": 2 * zz + q}

    def column(offset):
        return lax.rem(z + offset + NZ, NZ)

    def row_peer(i):
        return lax.rem(d + i, NDP)

    def copy(src, dst, send, recv, device):
        return pltpu.make_async_remote_copy(
            src_ref=src, dst_ref=dst, send_sem=send, recv_sem=recv, device_id=device, device_id_type=MESH
        )

    def signal(device):
        pl.semaphore_signal(barrier, inc=1, device_id=device, device_id_type=MESH)

    barrier = pltpu.get_barrier_semaphore()
    signal({"feat": partner})

    @pl.loop(1, NZ)
    def _(i):
        signal(chip(column(i)))

    @pl.loop(1, NDP)
    def _(i):
        signal({"dp": row_peer(i)})

    chunks = [feat_ref[:, LANES * i : LANES * (i + 1)].astype(F32) for i in range(16)]

    @pl.loop(0, GROUPS)
    def _(c):
        lanes = pl.ds(pl.multiple_of(c * LANES, LANES), LANES)

        block = lists_ref[:, lanes]
        total = jnp.zeros((16, LANES), F32)
        for k in range(K1):
            index = jnp.broadcast_to(block[k : k + 1], (16, LANES))
            low = lax.bitwise_and(index, 127)
            high = lax.shift_right_logical(index, 7)
            value = jnp.zeros((16, LANES), F32)
            for i in range(16):
                picked = jnp.take_along_axis(chunks[i], low, axis=1, mode="promise_in_bounds")
                value = jnp.where(high == i, picked, value)
            total += value
        xs[c, 0] = feat_ref[:, lanes]
        xs[c, 1] = (total / K1).astype(BF16)

    lane = iota((1, LANES), 1)
    slot = lax.rem(lane, 8)
    peer_rows = iota((NDP, LANES), 0) == iota((NDP, LANES), 1) // 8
    spread = (iota((8, LANES), 0) == lax.rem(iota((8, LANES), 1), 8)).astype(BF16)

    def flat(ref):
        wide = dot(ref[...].astype(F32).astype(BF16), spread)
        return jnp.sum(jnp.where(peer_rows, wide, 0.0), axis=0, keepdims=True)

    rows_own = flat(rows_ref)
    target_own = flat(target_ref)
    count_own = dot(count_ref[...].astype(F32).astype(BF16), peer_rows.astype(F32).astype(BF16))
    meta[d] = jnp.concatenate([rows_own, target_own, count_own, jnp.zeros((5, LANES), F32)], axis=0)

    pl.semaphore_wait(barrier, NZ - 1 + NDP - 1 + 1)

    xf[g] = xs[g]

    @pl.loop(1, GROUPS)
    def _(i):
        there = lax.rem(g + i, GROUPS)
        copy(xs.at[there], xf.at[g], far_s.at[i], far_r.at[g], chip(4 * there + zeta)).start()

    w_type = d // 8
    w_block = lax.rem(d // 2, 4)
    w_half = lax.rem(d, 2)
    w_lanes = pl.ds(pl.multiple_of(w_block * LANES, LANES), LANES)
    tile_rows = pl.ds(pl.multiple_of((lax.rem(zeta, 2) * 8 + g) * 16, 16), 16)
    sends_w = zeta // 2 == w_half

    @pl.when(sends_w & (w_type == 0))
    def _():
        w[d, tile_rows, :] = w1s_ref[:, w_lanes]

    @pl.when(sends_w & (w_type == 1))
    def _():
        w[d, tile_rows, :] = w1n_ref[:, w_lanes]

    def w_far(i):
        return copy(
            w.at[d, tile_rows, :], w.at[d, tile_rows, :], w1f_s.at[i], w1f_r.at[z], chip(column(i))
        )

    @pl.when(sends_w)
    def _():
        @pl.loop(1, NZ)
        def _(i):
            w_far(i).start()

    @pl.loop(1, NDP)
    def _(i):
        copy(meta.at[d], meta.at[d], meta_s.at[i], meta_r.at[d], {"dp": row_peer(i)}).start()

    swap_x = copy(xs, xp, d2d_s.at[0], d2d_r.at[0], {"feat": partner})
    swap_x.start()

    @pl.loop(1, NDP)
    def _(i):
        e = row_peer(i)
        copy(meta.at[e], meta.at[e], meta_s.at[i], meta_r.at[e], {"dp": e}).wait_recv()

    mine = iota((NDP, LANES), 1) // 8 == d
    same_slot = (lax.rem(iota((LANES, LANES), 0), 8) == lax.rem(iota((LANES, LANES), 1), 8)).astype(BF16)

    def from_peers(row):
        wide = dot(jnp.where(mine, meta[:, row, :], 0.0).astype(BF16), same_slot)
        return jnp.sum(jnp.where(peer_rows, wide, 0.0), axis=0, keepdims=True)

    rows_in = from_peers(0)
    target_in = from_peers(1)
    count_in = from_peers(2)
    slot_f = slot.astype(F32)
    base = (lane // 8 * 16).astype(F32)
    node = iota((16, LANES), 0).astype(F32)
    hits_in = jnp.where((target_own == node) & (slot_f < count_in), 1.0, 0.0)
    hits_out = jnp.where((rows_own == node) & (slot_f < count_own), 1.0, 0.0)
    everyone = iota((NDP * 16, LANES), 0).astype(F32)
    table_in = jnp.where(everyone == base + rows_in, 1.0, 0.0).astype(BF16)
    table_out = jnp.where(everyone == base + target_in, 1.0, 0.0).astype(BF16)
    mix_in = dot_nt(hits_in.astype(BF16), table_in).astype(BF16)
    mix_out = dot_nt(hits_out.astype(BF16), table_out).astype(BF16)
    degree = jnp.sum(hits_in, axis=1, keepdims=True)

    og = og_ref[...]
    grad_self = dot_nt(og, w2s_ref[...])
    grad_mean = dot_nt(og, w2n_ref[...]) / (1.0 + degree)
    gm_all[d] = grad_mean.astype(BF16)

    @pl.loop(1, NDP)
    def _(i):
        copy(gm_all.at[d], gm_all.at[d], gm_s.at[i], gm_r.at[d], {"dp": row_peer(i)}).start()

    swap_x.wait_recv()
    node_in = iota((1024, 512), 0)
    node_at = iota((1024, 512), 1)
    pick = jnp.where(node_in == 32 * (node_at // 16) + 16 * q + lax.rem(node_at, 16), 1.0, 0.0).astype(BF16)
    wide_rows = jnp.concatenate(
        [
            jnp.concatenate([buf[c, kind] for c in range(GROUPS)], axis=1)
            for buf in (xs, xp)
            for kind in (0, 1)
        ],
        axis=0,
    )
    x_cols = dot(wide_rows, pick).astype(BF16)

    @pl.loop(1, NDP)
    def _(i):
        e = row_peer(i)
        copy(gm_all.at[e], gm_all.at[e], gm_s.at[i], gm_r.at[e], {"dp": e}).wait_recv()

    back = dot(mix_out, gm_all[...].reshape(NDP * 16, 512))
    grad_hidden = grad_self + grad_mean + back

    @pl.loop(1, GROUPS)
    def _(i):
        there = lax.rem(g + i, GROUPS)
        copy(xf.at[there], xf.at[there], far_s.at[i], far_r.at[there], chip(4 * there + zeta)).wait_recv()

    for kind in (0, 1):
        turned = jnp.transpose(xf[:, kind].reshape(LANES, LANES).astype(F32)).astype(BF16)
        for i in range(4):
            xt[i, kind] = turned[32 * i : 32 * (i + 1)]
    xn[zeta] = xt[zeta]

    @pl.loop(1, 4)
    def _(i):
        there = lax.rem(zeta + i, 4)
        copy(xt.at[there], xn.at[zeta], near_s.at[i], near_r.at[zeta], chip(4 * g + there)).start()

    def w_source(i):
        from_zeta = 2 * w_half + i // 8
        from_g = lax.rem(i, 8)
        return 4 * from_g + from_zeta

    @pl.loop(0, 16)
    def _(i):
        source = w_source(i)
        at = pl.ds(pl.multiple_of(i * 16, 16), 16)

        @pl.when(source != z)
        def _():
            copy(w.at[d, at, :], w.at[d, at, :], w1f_s.at[0], w1f_r.at[source], chip(source)).wait_recv()

    @pl.loop(1, NDP)
    def _(i):
        copy(w.at[d], w.at[d], wd_s.at[i], wd_r.at[d], {"dp": row_peer(i)}).start()

    @pl.loop(1, 4)
    def _(i):
        there = lax.rem(zeta + i, 4)
        copy(xn.at[there], xn.at[there], near_s.at[i], near_r.at[there], chip(4 * g + there)).wait_recv()

    @pl.loop(1, NDP)
    def _(i):
        e = row_peer(i)
        copy(w.at[e], w.at[e], wd_s.at[i], wd_r.at[e], {"dp": e}).wait_recv()

    for block in range(4):
        total = jnp.zeros((32, LANES), F32)
        for kind in (0, 1):
            for half in (0, 1):
                x_part = jnp.concatenate([xn[2 * half, kind], xn[2 * half + 1, kind]], axis=1)
                total += dot(x_part, w[kind * 8 + block * 2 + half])
        part[0, :, LANES * block : LANES * (block + 1)] = total[:16]
        part[1, :, LANES * block : LANES * (block + 1)] = total[16:]

    swap_p = copy(part.at[1 - q], part_in, d2d_s.at[1], d2d_r.at[1], {"feat": partner})
    swap_p.start()
    swap_p.wait_recv()
    preact = part[q] + part_in[...]
    hidden = jnp.maximum(preact, 0.0).astype(BF16)
    gp[z] = jnp.where(preact > 0, grad_hidden, 0.0).astype(BF16)
    h_all[d] = hidden

    sent = []

    def pass_on(offset, targets):
        at = gp.at[column(offset)]
        for target in targets:
            c = copy(at, at, ag_s.at[len(sent)], ag_r.at[column(offset)], chip(column(target)))
            c.start()
            sent.append(c)

    def arrived(offset):
        at = gp.at[column(offset)]
        copy(at, at, ag_s.at[0], ag_r.at[column(offset)], chip(column(offset))).wait_recv()

    pass_on(*AG_PLAN[0])

    @pl.loop(1, NDP)
    def _(i):
        copy(h_all.at[d], h_all.at[d], h_s.at[i], h_r.at[d], {"dp": row_peer(i)}).start()

    for offset, targets in AG_PLAN[1:3]:
        arrived(offset)
        pass_on(offset, targets)

    @pl.loop(1, NDP)
    def _(i):
        e = row_peer(i)
        copy(h_all.at[e], h_all.at[e], h_s.at[i], h_r.at[e], {"dp": e}).wait_recv()

    neigh_sum = dot(mix_in, h_all[...].reshape(NDP * 16, 512))
    mean_two = ((hidden.astype(F32) + neigh_sum) / (1.0 + degree)).astype(BF16)
    out_ref[...] = (dot(hidden, w2s_ref[...]) + dot(mean_two, w2n_ref[...])).astype(BF16)

    for offset, targets in AG_PLAN[3:]:
        arrived(offset)
        pass_on(offset, targets)
    known = [offset % NZ for offset, _ in AG_PLAN]
    for offset in range(1, NZ):
        if offset not in known:
            arrived(offset)

    total = dot(x_cols, gp[...].reshape(NZ * 16, 512))
    res[...] = total
    swap_r = copy(res.at[32:64], res_in, d2d_s.at[2], d2d_r.at[2], {"feat": partner})
    swap_r.start()
    swap_r.wait_recv()
    gs_ref[...] = res[0:16] + res_in[0:16]
    gn_ref[...] = res[16:32] + res_in[16:32]

    for c in sent + [swap_x, swap_p, swap_r]:
        c.wait_send()

    @pl.loop(1, GROUPS)
    def _(i):
        there = lax.rem(g + i, GROUPS)
        copy(xs.at[there], xf.at[g], far_s.at[i], far_r.at[g], chip(4 * there + zeta)).wait_send()

    @pl.loop(1, 4)
    def _(i):
        there = lax.rem(zeta + i, 4)
        copy(xt.at[there], xn.at[zeta], near_s.at[i], near_r.at[zeta], chip(4 * g + there)).wait_send()

    @pl.when(sends_w)
    def _():
        @pl.loop(1, NZ)
        def _(i):
            w_far(i).wait_send()

    @pl.loop(1, NDP)
    def _(i):
        to = {"dp": row_peer(i)}
        copy(meta.at[d], meta.at[d], meta_s.at[i], meta_r.at[d], to).wait_send()
        copy(gm_all.at[d], gm_all.at[d], gm_s.at[i], gm_r.at[d], to).wait_send()
        copy(h_all.at[d], h_all.at[d], h_s.at[i], h_r.at[d], to).wait_send()
        copy(w.at[d], w.at[d], wd_s.at[i], wd_r.at[d], to).wait_send()


def on_device(
    features,
    neigh_lists,
    w1_self,
    w1_neigh,
    w2_self,
    w2_neigh,
    send_rows,
    send_count,
    recv_target,
    out_grad,
):
    dma = pltpu.SemaphoreType.DMA
    vmem = pl.BlockSpec(memory_space=pltpu.VMEM)
    layer_out, grad_self, grad_neigh = pl.pallas_call(
        kernel,
        out_shape=(
            jax.ShapeDtypeStruct((16, 512), BF16),
            jax.ShapeDtypeStruct((16, 512), F32),
            jax.ShapeDtypeStruct((16, 512), F32),
        ),
        in_specs=[vmem] * 10,
        out_specs=(vmem, vmem, vmem),
        scratch_shapes=[
            pltpu.VMEM((GROUPS, 2, 16, LANES), BF16),
            pltpu.VMEM((GROUPS, 2, 16, LANES), BF16),
            pltpu.VMEM((GROUPS, 2, 16, LANES), BF16),
            pltpu.VMEM((4, 2, 32, LANES), BF16),
            pltpu.VMEM((4, 2, 32, LANES), BF16),
            pltpu.VMEM((NDP, 256, LANES), BF16),
            pltpu.VMEM((NDP, 8, LANES), F32),
            pltpu.VMEM((NDP, 16, 512), BF16),
            pltpu.VMEM((NDP, 16, 512), BF16),
            pltpu.VMEM((NZ, 16, 512), BF16),
            pltpu.VMEM((2, 16, 512), F32),
            pltpu.VMEM((16, 512), F32),
            pltpu.VMEM((64, 512), F32),
            pltpu.VMEM((32, 512), F32),
            dma((NZ,)),
            dma((NZ,)),
            dma((GROUPS,)),
            dma((GROUPS,)),
            dma((4,)),
            dma((4,)),
            dma((NDP,)),
            dma((NDP,)),
            dma((NDP,)),
            dma((NDP,)),
            dma((NDP,)),
            dma((NDP,)),
            dma((NDP,)),
            dma((NDP,)),
            dma((NZ,)),
            dma((NZ,)),
            dma((3,)),
            dma((3,)),
        ],
        compiler_params=pltpu.CompilerParams(
            collective_id=0, has_side_effects=True, vmem_limit_bytes=40 * 1024 * 1024
        ),
    )(
        features[0],
        neigh_lists[0],
        w1_self,
        w1_neigh,
        w2_self,
        w2_neigh,
        send_rows[0, 0],
        send_count[0],
        recv_target[0, 0],
        out_grad[0, 0],
    )
    return layer_out[None, None], grad_self[None], grad_neigh[None]


def solution(mesh):
    in_specs = (
        P("dp", "feat", None),
        P("dp", None, None),
        P("feat", None),
        P("feat", None),
        P(),
        P(),
        P("dp", "feat", None, None),
        P("dp", "feat", None),
        P("dp", "feat", None, None),
        P("dp", "feat", None, None),
    )
    out_specs = (P("dp", "feat", None, None), P("dp", "feat", None), P("dp", "feat", None))
    return jax.shard_map(
        on_device, mesh=mesh, in_specs=in_specs, out_specs=out_specs, check_vma=False
    )
```

```python
import jax
import jax.numpy as jnp
from jax import lax
from jax.experimental import pallas as pl
from jax.experimental.pallas import tpu as pltpu
from jax.sharding import PartitionSpec as P

MESH = pl.DeviceIdType.MESH
K1 = 10
NZ = 32
NDP = 16
GROUPS = 8
LANES = 128
F32 = jnp.float32
BF16 = jnp.bfloat16

WINDOW_PLAN = (
    (0, (-8, 5, -5, 2, -2, 1, -1)),
    (5, (2, -2, 1, -1)),
    (-5, (2, -2, 1, -1)),
)


def place(offset):
    if offset <= -16:
        offset += NZ
    return offset + 7 if offset >= -7 else 16 - offset


def iota(shape, axis):
    return lax.broadcasted_iota(jnp.int32, shape, axis)


def dot(a, b):
    return jnp.dot(a, b, preferred_element_type=F32)


def dot_nt(a, b):
    return lax.dot_general(a, b, (((1,), (1,)), ((), ())), preferred_element_type=F32)


def kernel(
    feat_ref,
    lists_ref,
    w1s_ref,
    w1n_ref,
    w2s_hbm,
    w2n_hbm,
    rows_ref,
    count_ref,
    target_ref,
    og_ref,
    out_ref,
    gs_ref,
    gn_ref,
    w2s_ref,
    w2n_ref,
    xs,
    xp,
    tiles,
    slots,
    relay_up,
    relay_down,
    w,
    w_own,
    w_relay,
    meta,
    gm_all,
    h_all,
    gh_own,
    gh_relay,
    gh_opp,
    gp,
    part,
    part_in,
    res,
    res_in,
    local_s,
    x_s,
    x_r,
    relay_s,
    relay_r,
    wz_s,
    wz_r,
    wr_s,
    wr_r,
    wd_s,
    wd_r,
    meta_s,
    meta_r,
    gm_s,
    gm_r,
    h_s,
    h_r,
    gh_s,
    gh_r,
    gp_s,
    gp_r,
    d2d_s,
    d2d_r,
):
    f = lax.axis_index("feat")
    d = lax.axis_index("dp")
    z = f // 2
    q = lax.rem(f, 2)
    partner = {"feat": 2 * z + 1 - q}
    sends = []

    def chip(offset):
        return {"feat": 2 * lax.rem(z + offset + NZ, NZ) + q}

    def row_peer(i):
        return lax.rem(d + i, NDP)

    def copy(src, dst, send, recv, device):
        return pltpu.make_async_remote_copy(
            src_ref=src, dst_ref=dst, send_sem=send, recv_sem=recv, device_id=device, device_id_type=MESH
        )

    def send(src, dst, send_sem, recv_sem, device):
        c = copy(src, dst, send_sem, recv_sem, device)
        c.start()
        sends.append(c)
        return c

    def arrived(dst, recv_sem):
        copy(dst, dst, d2d_s.at[0], recv_sem, partner).wait_recv()

    def to_row(src, dst, send_sem, recv_sem):
        @pl.loop(1, NDP)
        def _(i):
            copy(src, dst, send_sem.at[i], recv_sem.at[d], {"dp": row_peer(i)}).start()

    def from_row(buf, recv_sem):
        @pl.loop(1, NDP)
        def _(i):
            e = row_peer(i)
            arrived(buf.at[e], recv_sem.at[e])

    barrier = pltpu.get_barrier_semaphore()

    def signal(device):
        pl.semaphore_signal(barrier, inc=1, device_id=device, device_id_type=MESH)

    for offset in range(8, 0, -1):
        signal(chip(offset))
        signal(chip(-offset))
    signal(partner)

    @pl.loop(1, NDP)
    def _(i):
        signal({"dp": row_peer(i)})

    get_w2s = pltpu.make_async_copy(w2s_hbm, w2s_ref, local_s.at[0])
    get_w2n = pltpu.make_async_copy(w2n_hbm, w2n_ref, local_s.at[1])
    get_w2s.start()
    get_w2n.start()

    chunks = [feat_ref[:, LANES * i : LANES * (i + 1)].astype(F32) for i in range(16)]

    @pl.loop(0, GROUPS)
    def _(c):
        lanes = pl.ds(pl.multiple_of(c * LANES, LANES), LANES)
        total = jnp.zeros((16, LANES), F32)
        for k in range(K1):
            index = jnp.broadcast_to(lists_ref[k, :, lanes], (16, LANES))
            low = lax.bitwise_and(index, 127)
            high = lax.shift_right_logical(index, 7)
            value = jnp.zeros((16, LANES), F32)
            for i in range(16):
                picked = jnp.take_along_axis(chunks[i], low, axis=1, mode="promise_in_bounds")
                value = jnp.where(high == i, picked, value)
            total += value
        xs[c, 0] = feat_ref[:, lanes]
        xs[c, 1] = (total / K1).astype(BF16)

    quarter = iota((16, LANES), 1) // 32

    @pl.loop(0, GROUPS)
    def _(c):
        far = lax.rem(c + 4, GROUPS)
        parts = [xs[c, 0], xs[c, 1], xs[far, 0], xs[far, 1]]
        parts = [p.astype(F32) for p in parts]
        for i in range(4):
            tile = jnp.zeros((16, LANES), F32)
            for k in range(4):
                shift = (32 * (k - i)) % LANES
                moved = pltpu.roll(parts[k], shift, 1) if shift else parts[k]
                tile = jnp.where(quarter == k, moved, tile)
            tiles[lax.rem(4 * c + i - z + NZ, NZ)] = tile.astype(BF16)

    slots[place(0)] = tiles[0]

    lane = iota((1, LANES), 1)
    slot = lax.rem(lane, 8)
    peer_rows = iota((NDP, LANES), 0) == iota((NDP, LANES), 1) // 8
    spread = peer_rows.astype(F32).astype(BF16)
    own_slot = iota((8, LANES), 0) == lax.rem(iota((8, LANES), 1), 8)

    def flat(ref):
        wide = dot(ref[...].astype(F32).astype(BF16), spread)
        return jnp.sum(jnp.where(own_slot, wide, 0.0), axis=0, keepdims=True)

    rows_own = flat(rows_ref)
    target_own = flat(target_ref)
    count_own = dot(count_ref[...].astype(F32).astype(BF16), spread)
    meta[d] = jnp.concatenate([rows_own, target_own, count_own, jnp.zeros((5, LANES), F32)], axis=0)

    piece = lax.rem(d, 8)
    w_lanes = pl.ds(pl.multiple_of(lax.rem(d, 4) * LANES, LANES), LANES)
    near_column = d < 8
    own_tile = jnp.where(piece < 4, w1s_ref[:, w_lanes].astype(F32), w1n_ref[:, w_lanes].astype(F32)).astype(BF16)
    w_own[...] = own_tile

    @pl.when(near_column)
    def _():
        w[d, pl.ds(16 * place(0), 16), :] = own_tile

    def w_at(offset):
        return w.at[d, pl.ds(16 * (place(offset) % 16), 16), :]

    pl.semaphore_wait(barrier, 16 + 1 + NDP - 1)

    send(tiles.at[pl.ds(9, 8)], relay_up, relay_s.at[0], relay_r.at[0], chip(8))
    send(tiles.at[pl.ds(17, 7)], relay_down, relay_s.at[1], relay_r.at[1], chip(-8))

    w_near = [t for k in range(8, 0, -1) for t in (-k, k) if t != 8]
    w_near_sends = [
        copy(w_own, w_at(-t), wz_s.at[n], wz_r.at[place(-t) % 16], chip(t)) for n, t in enumerate(w_near)
    ]
    w_up = copy(w_own, w_at(-8), wr_s.at[0], wz_r.at[place(-8) % 16], chip(8))
    w_down = copy(w_own, w_relay, wr_s.at[1], wr_r.at[0], chip(-8))
    w_far_sends = [
        copy(w_at(-8), w_at(-8 - t), wz_s.at[t - 1], wz_r.at[place(-8 - t) % 16], chip(t)) for t in range(8, 0, -1)
    ] + [
        copy(w_relay, w_at(8 + t), wz_s.at[7 + t], wz_r.at[place(8 + t) % 16], chip(-t)) for t in range(7, 0, -1)
    ]

    @pl.when(jnp.logical_not(near_column))
    def _():
        w_up.start()
        w_down.start()

    for k in range(8, 0, -1):
        for t in (k, -k):
            send(tiles.at[t % NZ], slots.at[place(-t)], x_s.at[t + 8], x_r.at[place(-t)], chip(t))

    @pl.when(near_column)
    def _():
        for c in w_near_sends:
            c.start()

    to_row(meta.at[d], meta.at[d], meta_s, meta_r)
    send(xs, xp, d2d_s.at[0], d2d_r.at[0], partner)

    from_row(meta, meta_r)
    mine = iota((NDP, LANES), 1) // 8 == d
    same_slot = (lax.rem(iota((LANES, LANES), 0), 8) == lax.rem(iota((LANES, LANES), 1), 8)).astype(BF16)

    def from_peers(row):
        wide = dot(jnp.where(mine, meta[:, row, :], 0.0).astype(BF16), same_slot)
        return jnp.sum(jnp.where(peer_rows, wide, 0.0), axis=0, keepdims=True)

    rows_in = from_peers(0)
    target_in = from_peers(1)
    count_in = from_peers(2)
    slot_f = slot.astype(F32)
    base = (lane // 8 * 16).astype(F32)
    node = iota((16, LANES), 0).astype(F32)
    hits_in = jnp.where((target_own == node) & (slot_f < count_in), 1.0, 0.0)
    degree = jnp.sum(hits_in, axis=1, keepdims=True)

    og = og_ref[...]
    get_w2n.wait()
    grad_mean = dot_nt(og, w2n_ref[...]) / (1.0 + degree)
    gm_all[d] = grad_mean.astype(BF16)
    to_row(gm_all.at[d], gm_all.at[d], gm_s, gm_r)

    get_w2s.wait()
    grad_self = dot_nt(og, w2s_ref[...])
    hits_out = jnp.where((rows_own == node) & (slot_f < count_own), 1.0, 0.0)
    everyone = iota((NDP * 16, LANES), 0).astype(F32)
    table_in = jnp.where(everyone == base + rows_in, 1.0, 0.0).astype(BF16)
    table_out = jnp.where(everyone == base + target_in, 1.0, 0.0).astype(BF16)
    mix_in = dot_nt(hits_in.astype(BF16), table_in).astype(BF16)
    mix_out = dot_nt(hits_out.astype(BF16), table_out).astype(BF16)

    @pl.when(jnp.logical_not(near_column))
    def _():
        arrived(w_at(-8), wz_r.at[place(-8) % 16])
        arrived(w_relay, wr_r.at[0])
        for c in w_far_sends:
            c.start()

    arrived(relay_up, relay_r.at[0])
    for t in range(8, 0, -1):
        send(relay_up.at[t - 1], slots.at[place(-8 - t)], x_s.at[16 + t], x_r.at[place(-8 - t)], chip(t))
    arrived(relay_down, relay_r.at[1])
    for t in range(7, 0, -1):
        send(relay_down.at[7 - t], slots.at[place(8 + t)], x_s.at[24 + t], x_r.at[place(8 + t)], chip(-t))

    @pl.when(near_column)
    def _():
        for t in w_near:
            arrived(w_at(-t), wz_r.at[place(-t) % 16])
        to_row(w.at[d], w.at[d], wd_s, wd_r)

    from_row(gm_all, gm_r)
    back = dot(mix_out, gm_all[...].reshape(NDP * 16, 512))
    gh_own[...] = (grad_self + grad_mean + back).astype(BF16)
    send(gh_own, gh_relay, gh_s.at[0], gh_r.at[0], chip(8))

    arrived(xp, d2d_r.at[0])
    node_in = iota((1024, 512), 0)
    node_at = iota((1024, 512), 1)
    block_at = node_at // 16
    chip_at = lax.rem(z - 7 + NZ + block_at // 2 + 16 * lax.rem(block_at, 2), NZ)
    pick = jnp.where(node_in == 32 * chip_at + 16 * q + lax.rem(node_at, 16), 1.0, 0.0).astype(BF16)
    wide_rows = jnp.concatenate(
        [
            jnp.concatenate([buf[c, kind] for c in range(GROUPS)], axis=1)
            for buf in (xs, xp)
            for kind in (0, 1)
        ],
        axis=0,
    )
    x_cols = dot(wide_rows, pick).astype(BF16)

    @pl.when(jnp.logical_not(near_column))
    def _():
        for offset in list(range(9, 17)) + list(range(-15, -8)):
            arrived(w_at(offset), wz_r.at[place(offset) % 16])
        to_row(w.at[d], w.at[d], wd_s, wd_r)

    arrived(gh_relay, gh_r.at[0])
    send(gh_relay, gh_opp, gh_s.at[1], gh_r.at[1], chip(8))

    for offset in range(-15, 17):
        if offset:
            arrived(slots.at[place(offset)], x_r.at[place(offset)])
    turned = [
        jnp.transpose(slots[16 * half : 16 * half + 16].reshape(256, LANES).astype(F32)).astype(BF16)
        for half in (0, 1)
    ]

    def rows_of(half, kind):
        t = turned[half]
        return jnp.concatenate([t[32 * kind : 32 * kind + 32], t[64 + 32 * kind : 96 + 32 * kind]], axis=0)

    x_rows = [[rows_of(half, kind) for kind in (0, 1)] for half in (0, 1)]

    from_row(w, wd_r)
    for block in range(4):
        total = jnp.zeros((64, LANES), F32)
        for half in (0, 1):
            for kind in (0, 1):
                total += dot(x_rows[half][kind], w[half * 8 + kind * 4 + block])
        lanes = slice(LANES * block, LANES * (block + 1))
        for core in (0, 1):
            part[core, 0:16, lanes] = total[16 * core : 16 * core + 16]
            part[core, 16:32, lanes] = total[32 + 16 * core : 48 + 16 * core]

    send(part.at[1 - q], part_in, d2d_s.at[1], d2d_r.at[1], partner)
    arrived(part_in, d2d_r.at[1])
    preact = part[q] + part_in[...]
    hidden = jnp.maximum(preact[0:16], 0.0).astype(BF16)
    arrived(gh_opp, gh_r.at[1])
    gp[7, 0] = jnp.where(preact[0:16] > 0, gh_own[...].astype(F32), 0.0).astype(BF16)
    gp[7, 1] = jnp.where(preact[16:32] > 0, gh_opp[...].astype(F32), 0.0).astype(BF16)
    h_all[d] = hidden

    def pass_on(offset, targets):
        for target in targets:
            there = offset - target + 7
            send(gp.at[offset + 7], gp.at[there], gp_s.at[there], gp_r.at[there], chip(target))

    pass_on(*WINDOW_PLAN[0])
    to_row(h_all.at[d], h_all.at[d], h_s, h_r)
    for offset, targets in WINDOW_PLAN[1:]:
        arrived(gp.at[offset + 7], gp_r.at[offset + 7])
        pass_on(offset, targets)

    from_row(h_all, h_r)
    neigh_sum = dot(mix_in, h_all[...].reshape(NDP * 16, 512))
    mean_two = ((hidden.astype(F32) + neigh_sum) / (1.0 + degree)).astype(BF16)
    out_ref[...] = (dot(hidden, w2s_ref[...]) + dot(mean_two, w2n_ref[...])).astype(BF16)

    for offset in range(-7, 9):
        if offset not in (0, 5, -5):
            arrived(gp.at[offset + 7], gp_r.at[offset + 7])

    res[...] = dot(x_cols, gp[...].reshape(512, 512))
    send(res.at[32:64], res_in, d2d_s.at[2], d2d_r.at[2], partner)
    arrived(res_in, d2d_r.at[2])
    gs_ref[...] = res[0:16] + res_in[0:16]
    gn_ref[...] = res[16:32] + res_in[16:32]

    for c in sends:
        c.wait_send()

    @pl.when(near_column)
    def _():
        for c in w_near_sends:
            c.wait_send()

    @pl.when(jnp.logical_not(near_column))
    def _():
        for c in [w_up, w_down] + w_far_sends:
            c.wait_send()

    @pl.loop(1, NDP)
    def _(i):
        to = {"dp": row_peer(i)}
        copy(meta.at[d], meta.at[d], meta_s.at[i], meta_r.at[d], to).wait_send()
        copy(gm_all.at[d], gm_all.at[d], gm_s.at[i], gm_r.at[d], to).wait_send()
        copy(h_all.at[d], h_all.at[d], h_s.at[i], h_r.at[d], to).wait_send()
        copy(w.at[d], w.at[d], wd_s.at[i], wd_r.at[d], to).wait_send()


def on_device(
    features,
    neigh_lists,
    w1_self,
    w1_neigh,
    w2_self,
    w2_neigh,
    send_rows,
    send_count,
    recv_target,
    out_grad,
):
    dma = pltpu.SemaphoreType.DMA
    vmem = pl.BlockSpec(memory_space=pltpu.VMEM)
    hbm = pl.BlockSpec(memory_space=pl.ANY)
    layer_out, grad_self, grad_neigh = pl.pallas_call(
        kernel,
        out_shape=(
            jax.ShapeDtypeStruct((16, 512), BF16),
            jax.ShapeDtypeStruct((16, 512), F32),
            jax.ShapeDtypeStruct((16, 512), F32),
        ),
        in_specs=[vmem] * 4 + [hbm] * 2 + [vmem] * 4,
        out_specs=(vmem, vmem, vmem),
        scratch_shapes=[
            pltpu.VMEM((512, 512), BF16),
            pltpu.VMEM((512, 512), BF16),
            pltpu.VMEM((GROUPS, 2, 16, LANES), BF16),
            pltpu.VMEM((GROUPS, 2, 16, LANES), BF16),
            pltpu.VMEM((NZ, 16, LANES), BF16),
            pltpu.VMEM((NZ, 16, LANES), BF16),
            pltpu.VMEM((8, 16, LANES), BF16),
            pltpu.VMEM((7, 16, LANES), BF16),
            pltpu.VMEM((NDP, 256, LANES), BF16),
            pltpu.VMEM((16, LANES), BF16),
            pltpu.VMEM((16, LANES), BF16),
            pltpu.VMEM((NDP, 8, LANES), F32),
            pltpu.VMEM((NDP, 16, 512), BF16),
            pltpu.VMEM((NDP, 16, 512), BF16),
            pltpu.VMEM((16, 512), BF16),
            pltpu.VMEM((16, 512), BF16),
            pltpu.VMEM((16, 512), BF16),
            pltpu.VMEM((16, 2, 16, 512), BF16),
            pltpu.VMEM((2, 32, 512), F32),
            pltpu.VMEM((32, 512), F32),
            pltpu.VMEM((64, 512), F32),
            pltpu.VMEM((32, 512), F32),
            dma((2,)),
            dma((NZ,)),
            dma((NZ,)),
            dma((2,)),
            dma((2,)),
            dma((16,)),
            dma((16,)),
            dma((2,)),
            dma((1,)),
            dma((NDP,)),
            dma((NDP,)),
            dma((NDP,)),
            dma((NDP,)),
            dma((NDP,)),
            dma((NDP,)),
            dma((NDP,)),
            dma((NDP,)),
            dma((2,)),
            dma((2,)),
            dma((16,)),
            dma((16,)),
            dma((3,)),
            dma((3,)),
        ],
        compiler_params=pltpu.CompilerParams(
            collective_id=0, has_side_effects=True, vmem_limit_bytes=40 * 1024 * 1024
        ),
    )(
        features[0],
        jnp.transpose(neigh_lists, (1, 0, 2)),
        w1_self,
        w1_neigh,
        w2_self,
        w2_neigh,
        jnp.transpose(send_rows[0, 0]),
        send_count[0],
        jnp.transpose(recv_target[0, 0]),
        out_grad[0, 0],
    )
    return layer_out[None, None], grad_self[None], grad_neigh[None]


def solution(mesh):
    in_specs = (
        P("dp", "feat", None),
        P("dp", None, None),
        P("feat", None),
        P("feat", None),
        P(),
        P(),
        P("dp", "feat", None, None),
        P("dp", "feat", None),
        P("dp", "feat", None, None),
        P("dp", "feat", None, None),
    )
    out_specs = (P("dp", "feat", None, None), P("dp", "feat", None), P("dp", "feat", None))
    return jax.shard_map(
        on_device, mesh=mesh, in_specs=in_specs, out_specs=out_specs, check_vma=False
    )
```

```python
import jax
import jax.numpy as jnp
from jax import lax
from jax.experimental import pallas as pl
from jax.experimental.pallas import tpu as pltpu
from jax.sharding import PartitionSpec as P

MESH = pl.DeviceIdType.MESH
K1 = 10
NZ = 32
NDP = 16
GROUPS = 8
LANES = 128
F32 = jnp.float32
BF16 = jnp.bfloat16

WINDOW_PLAN = (
    (0, (-8, 5, -5, 2, -2, 1, -1)),
    (5, (2, -2, 1, -1)),
    (-5, (2, -2, 1, -1)),
)


def place(offset):
    if offset <= -16:
        offset += NZ
    return offset + 7 if offset >= -7 else 16 - offset


def iota(shape, axis):
    return lax.broadcasted_iota(jnp.int32, shape, axis)


def dot(a, b):
    return jnp.dot(a, b, preferred_element_type=F32)


def dot_nt(a, b):
    return lax.dot_general(a, b, (((1,), (1,)), ((), ())), preferred_element_type=F32)


def kernel(
    feat_in,
    lists_in,
    w1s_in,
    w1n_in,
    w2s_in,
    w2n_in,
    rows_in_hbm,
    count_in_hbm,
    target_in_hbm,
    og_in,
    out_hbm,
    gs_hbm,
    gn_hbm,
    feat_ref,
    lists_ref,
    w1s_ref,
    w1n_ref,
    w2s_ref,
    w2n_ref,
    rows_ref,
    count_ref,
    target_ref,
    og_ref,
    out_ref,
    gs_ref,
    gn_ref,
    xs,
    xp,
    tiles,
    slots,
    relay_up,
    relay_down,
    w,
    w_own,
    w_relay,
    meta,
    gm_all,
    h_all,
    gh_own,
    gh_relay,
    gh_opp,
    gp,
    part,
    part_in,
    res,
    res_in,
    local_s,
    x_s,
    x_r,
    relay_s,
    relay_r,
    wz_s,
    wz_r,
    wr_s,
    wr_r,
    wd_s,
    wd_r,
    meta_s,
    meta_r,
    gm_s,
    gm_r,
    h_s,
    h_r,
    gh_s,
    gh_r,
    gp_s,
    gp_r,
    d2d_s,
    d2d_r,
):
    f = lax.axis_index("feat")
    d = lax.axis_index("dp")
    z = f // 2
    q = lax.rem(f, 2)
    partner = {"feat": 2 * z + 1 - q}
    sends = []

    def chip(offset):
        return {"feat": 2 * lax.rem(z + offset + NZ, NZ) + q}

    def row_peer(i):
        return lax.rem(d + i, NDP)

    def copy(src, dst, send, recv, device):
        return pltpu.make_async_remote_copy(
            src_ref=src, dst_ref=dst, send_sem=send, recv_sem=recv, device_id=device, device_id_type=MESH
        )

    def send(src, dst, send_sem, recv_sem, device):
        c = copy(src, dst, send_sem, recv_sem, device)
        c.start()
        sends.append(c)
        return c

    def arrived(dst, recv_sem):
        copy(dst, dst, d2d_s.at[0], recv_sem, partner).wait_recv()

    def to_row(src, dst, send_sem, recv_sem):
        @pl.loop(1, NDP)
        def _(i):
            copy(src, dst, send_sem.at[i], recv_sem.at[d], {"dp": row_peer(i)}).start()

    def from_row(buf, recv_sem):
        @pl.loop(1, NDP)
        def _(i):
            e = row_peer(i)
            arrived(buf.at[e], recv_sem.at[e])

    pairs = (
        (feat_in, feat_ref),
        (lists_in, lists_ref),
        (rows_in_hbm, rows_ref),
        (count_in_hbm, count_ref),
        (target_in_hbm, target_ref),
        (w1s_in, w1s_ref),
        (w1n_in, w1n_ref),
        (og_in, og_ref),
        (w2n_in, w2n_ref),
        (w2s_in, w2s_ref),
    )
    loads = [pltpu.make_async_copy(src, dst, local_s.at[n]) for n, (src, dst) in enumerate(pairs)]
    for c in loads[:2]:
        c.start()

    barrier = pltpu.get_barrier_semaphore()

    def signal(device):
        pl.semaphore_signal(barrier, inc=1, device_id=device, device_id_type=MESH)

    for offset in range(8, 0, -1):
        signal(chip(offset))
        signal(chip(-offset))
    signal(partner)

    @pl.loop(1, NDP)
    def _(i):
        signal({"dp": row_peer(i)})

    for c in loads[2:]:
        c.start()
    for c in loads[:2]:
        c.wait()

    chunks = [feat_ref[:, LANES * i : LANES * (i + 1)].astype(F32) for i in range(16)]

    @pl.loop(0, GROUPS)
    def _(c):
        lanes = pl.ds(pl.multiple_of(c * LANES, LANES), LANES)
        total = jnp.zeros((16, LANES), F32)
        for k in range(K1):
            index = jnp.broadcast_to(lists_ref[k, :, lanes], (16, LANES))
            low = lax.bitwise_and(index, 127)
            high = lax.shift_right_logical(index, 7)
            value = jnp.zeros((16, LANES), F32)
            for i in range(16):
                picked = jnp.take_along_axis(chunks[i], low, axis=1, mode="promise_in_bounds")
                value = jnp.where(high == i, picked, value)
            total += value
        xs[c, 0] = feat_ref[:, lanes]
        xs[c, 1] = (total / K1).astype(BF16)

    quarter = iota((16, LANES), 1) // 32

    @pl.loop(0, GROUPS)
    def _(c):
        far = lax.rem(c + 4, GROUPS)
        parts = [xs[c, 0], xs[c, 1], xs[far, 0], xs[far, 1]]
        parts = [p.astype(F32) for p in parts]
        for i in range(4):
            tile = jnp.zeros((16, LANES), F32)
            for k in range(4):
                shift = (32 * (k - i)) % LANES
                moved = pltpu.roll(parts[k], shift, 1) if shift else parts[k]
                tile = jnp.where(quarter == k, moved, tile)
            tiles[lax.rem(4 * c + i - z + NZ, NZ)] = tile.astype(BF16)

    slots[place(0)] = tiles[0]

    lane = iota((1, LANES), 1)
    slot = lax.rem(lane, 8)
    peer_rows = iota((NDP, LANES), 0) == iota((NDP, LANES), 1) // 8
    spread = peer_rows.astype(F32).astype(BF16)
    own_slot = iota((8, LANES), 0) == lax.rem(iota((8, LANES), 1), 8)

    for c in loads[2:7]:
        c.wait()

    def flat(ref):
        wide = dot(ref[...].astype(F32).astype(BF16), spread)
        return jnp.sum(jnp.where(own_slot, wide, 0.0), axis=0, keepdims=True)

    rows_own = flat(rows_ref)
    target_own = flat(target_ref)
    count_own = dot(count_ref[...].astype(F32).astype(BF16), spread)
    meta[d] = jnp.concatenate([rows_own, target_own, count_own, jnp.zeros((5, LANES), F32)], axis=0)

    piece = lax.rem(d, 8)
    w_lanes = pl.ds(pl.multiple_of(lax.rem(d, 4) * LANES, LANES), LANES)
    near_column = d < 8
    own_tile = jnp.where(piece < 4, w1s_ref[:, w_lanes].astype(F32), w1n_ref[:, w_lanes].astype(F32)).astype(BF16)
    w_own[...] = own_tile

    @pl.when(near_column)
    def _():
        w[d, pl.ds(16 * place(0), 16), :] = own_tile

    def w_at(offset):
        return w.at[d, pl.ds(16 * (place(offset) % 16), 16), :]

    pl.semaphore_wait(barrier, 16 + 1 + NDP - 1)

    send(tiles.at[pl.ds(9, 8)], relay_up, relay_s.at[0], relay_r.at[0], chip(8))
    send(tiles.at[pl.ds(17, 7)], relay_down, relay_s.at[1], relay_r.at[1], chip(-8))

    w_near = [t for k in range(8, 0, -1) for t in (-k, k) if t != 8]
    w_near_sends = [
        copy(w_own, w_at(-t), wz_s.at[n], wz_r.at[place(-t) % 16], chip(t)) for n, t in enumerate(w_near)
    ]
    w_up = copy(w_own, w_at(-8), wr_s.at[0], wz_r.at[place(-8) % 16], chip(8))
    w_down = copy(w_own, w_relay, wr_s.at[1], wr_r.at[0], chip(-8))
    w_far_sends = [
        copy(w_at(-8), w_at(-8 - t), wz_s.at[t - 1], wz_r.at[place(-8 - t) % 16], chip(t)) for t in range(8, 0, -1)
    ] + [
        copy(w_relay, w_at(8 + t), wz_s.at[7 + t], wz_r.at[place(8 + t) % 16], chip(-t)) for t in range(7, 0, -1)
    ]

    @pl.when(jnp.logical_not(near_column))
    def _():
        w_up.start()
        w_down.start()

    for k in range(8, 0, -1):
        for t in (k, -k):
            send(tiles.at[t % NZ], slots.at[place(-t)], x_s.at[t + 8], x_r.at[place(-t)], chip(t))

    @pl.when(near_column)
    def _():
        for c in w_near_sends:
            c.start()

    to_row(meta.at[d], meta.at[d], meta_s, meta_r)
    send(xs, xp, d2d_s.at[0], d2d_r.at[0], partner)

    from_row(meta, meta_r)
    mine = iota((NDP, LANES), 1) // 8 == d
    same_slot = (lax.rem(iota((LANES, LANES), 0), 8) == lax.rem(iota((LANES, LANES), 1), 8)).astype(BF16)

    def from_peers(row):
        wide = dot(jnp.where(mine, meta[:, row, :], 0.0).astype(BF16), same_slot)
        return jnp.sum(jnp.where(peer_rows, wide, 0.0), axis=0, keepdims=True)

    rows_in = from_peers(0)
    target_in = from_peers(1)
    count_in = from_peers(2)
    slot_f = slot.astype(F32)
    base = (lane // 8 * 16).astype(F32)
    node = iota((16, LANES), 0).astype(F32)
    hits_in = jnp.where((target_own == node) & (slot_f < count_in), 1.0, 0.0)
    degree = jnp.sum(hits_in, axis=1, keepdims=True)

    loads[7].wait()
    loads[8].wait()
    og = og_ref[...]
    grad_mean = dot_nt(og, w2n_ref[...]) / (1.0 + degree)
    gm_all[d] = grad_mean.astype(BF16)
    to_row(gm_all.at[d], gm_all.at[d], gm_s, gm_r)

    loads[9].wait()
    grad_self = dot_nt(og, w2s_ref[...])
    hits_out = jnp.where((rows_own == node) & (slot_f < count_own), 1.0, 0.0)
    everyone = iota((NDP * 16, LANES), 0).astype(F32)
    table_in = jnp.where(everyone == base + rows_in, 1.0, 0.0).astype(BF16)
    table_out = jnp.where(everyone == base + target_in, 1.0, 0.0).astype(BF16)
    mix_in = dot_nt(hits_in.astype(BF16), table_in).astype(BF16)
    mix_out = dot_nt(hits_out.astype(BF16), table_out).astype(BF16)

    @pl.when(jnp.logical_not(near_column))
    def _():
        arrived(w_at(-8), wz_r.at[place(-8) % 16])
        arrived(w_relay, wr_r.at[0])
        for c in w_far_sends:
            c.start()

    arrived(relay_up, relay_r.at[0])
    for t in range(8, 0, -1):
        send(relay_up.at[t - 1], slots.at[place(-8 - t)], x_s.at[16 + t], x_r.at[place(-8 - t)], chip(t))
    arrived(relay_down, relay_r.at[1])
    for t in range(7, 0, -1):
        send(relay_down.at[7 - t], slots.at[place(8 + t)], x_s.at[24 + t], x_r.at[place(8 + t)], chip(-t))

    @pl.when(near_column)
    def _():
        for t in w_near:
            arrived(w_at(-t), wz_r.at[place(-t) % 16])
        to_row(w.at[d], w.at[d], wd_s, wd_r)

    from_row(gm_all, gm_r)
    back = dot(mix_out, gm_all[...].reshape(NDP * 16, 512))
    gh_own[...] = (grad_self + grad_mean + back).astype(BF16)
    send(gh_own, gh_relay, gh_s.at[0], gh_r.at[0], chip(8))

    arrived(xp, d2d_r.at[0])
    node_in = iota((1024, 512), 0)
    node_at = iota((1024, 512), 1)
    block_at = node_at // 16
    chip_at = lax.rem(z - 7 + NZ + block_at // 2 + 16 * lax.rem(block_at, 2), NZ)
    pick = jnp.where(node_in == 32 * chip_at + 16 * q + lax.rem(node_at, 16), 1.0, 0.0).astype(BF16)
    wide_rows = jnp.concatenate(
        [
            jnp.concatenate([buf[c, kind] for c in range(GROUPS)], axis=1)
            for buf in (xs, xp)
            for kind in (0, 1)
        ],
        axis=0,
    )
    x_cols = dot(wide_rows, pick).astype(BF16)

    @pl.when(jnp.logical_not(near_column))
    def _():
        for offset in list(range(9, 17)) + list(range(-15, -8)):
            arrived(w_at(offset), wz_r.at[place(offset) % 16])
        to_row(w.at[d], w.at[d], wd_s, wd_r)

    arrived(gh_relay, gh_r.at[0])
    send(gh_relay, gh_opp, gh_s.at[1], gh_r.at[1], chip(8))

    for offset in range(-15, 17):
        if offset:
            arrived(slots.at[place(offset)], x_r.at[place(offset)])
    turned = [
        jnp.transpose(slots[16 * half : 16 * half + 16].reshape(256, LANES).astype(F32)).astype(BF16)
        for half in (0, 1)
    ]

    def rows_of(half, kind):
        t = turned[half]
        return jnp.concatenate([t[32 * kind : 32 * kind + 32], t[64 + 32 * kind : 96 + 32 * kind]], axis=0)

    x_rows = [[rows_of(half, kind) for kind in (0, 1)] for half in (0, 1)]

    from_row(w, wd_r)
    for block in range(4):
        total = jnp.zeros((64, LANES), F32)
        for half in (0, 1):
            for kind in (0, 1):
                total += dot(x_rows[half][kind], w[half * 8 + kind * 4 + block])
        lanes = slice(LANES * block, LANES * (block + 1))
        for core in (0, 1):
            part[core, 0:16, lanes] = total[16 * core : 16 * core + 16]
            part[core, 16:32, lanes] = total[32 + 16 * core : 48 + 16 * core]

    send(part.at[1 - q], part_in, d2d_s.at[1], d2d_r.at[1], partner)
    arrived(part_in, d2d_r.at[1])
    preact = part[q] + part_in[...]
    hidden = jnp.maximum(preact[0:16], 0.0).astype(BF16)
    arrived(gh_opp, gh_r.at[1])
    gp[7, 0] = jnp.where(preact[0:16] > 0, gh_own[...].astype(F32), 0.0).astype(BF16)
    gp[7, 1] = jnp.where(preact[16:32] > 0, gh_opp[...].astype(F32), 0.0).astype(BF16)
    h_all[d] = hidden

    def pass_on(offset, targets):
        for target in targets:
            there = offset - target + 7
            send(gp.at[offset + 7], gp.at[there], gp_s.at[there], gp_r.at[there], chip(target))

    pass_on(*WINDOW_PLAN[0])
    to_row(h_all.at[d], h_all.at[d], h_s, h_r)
    for offset, targets in WINDOW_PLAN[1:]:
        arrived(gp.at[offset + 7], gp_r.at[offset + 7])
        pass_on(offset, targets)

    from_row(h_all, h_r)
    stores = [
        pltpu.make_async_copy(src, dst, local_s.at[10 + n])
        for n, (src, dst) in enumerate(((out_ref, out_hbm), (gs_ref, gs_hbm), (gn_ref, gn_hbm)))
    ]
    neigh_sum = dot(mix_in, h_all[...].reshape(NDP * 16, 512))
    mean_two = ((hidden.astype(F32) + neigh_sum) / (1.0 + degree)).astype(BF16)
    out_ref[...] = (dot(hidden, w2s_ref[...]) + dot(mean_two, w2n_ref[...])).astype(BF16)
    stores[0].start()

    for offset in range(-7, 9):
        if offset not in (0, 5, -5):
            arrived(gp.at[offset + 7], gp_r.at[offset + 7])

    res[...] = dot(x_cols, gp[...].reshape(512, 512))
    send(res.at[32:64], res_in, d2d_s.at[2], d2d_r.at[2], partner)
    arrived(res_in, d2d_r.at[2])
    gs_ref[...] = res[0:16] + res_in[0:16]
    gn_ref[...] = res[16:32] + res_in[16:32]

    stores[1].start()
    stores[2].start()

    for c in sends:
        c.wait_send()

    @pl.when(near_column)
    def _():
        for c in w_near_sends:
            c.wait_send()

    @pl.when(jnp.logical_not(near_column))
    def _():
        for c in [w_up, w_down] + w_far_sends:
            c.wait_send()

    @pl.loop(1, NDP)
    def _(i):
        to = {"dp": row_peer(i)}
        copy(meta.at[d], meta.at[d], meta_s.at[i], meta_r.at[d], to).wait_send()
        copy(gm_all.at[d], gm_all.at[d], gm_s.at[i], gm_r.at[d], to).wait_send()
        copy(h_all.at[d], h_all.at[d], h_s.at[i], h_r.at[d], to).wait_send()
        copy(w.at[d], w.at[d], wd_s.at[i], wd_r.at[d], to).wait_send()

    for c in stores:
        c.wait()


def on_device(
    features,
    neigh_lists,
    w1_self,
    w1_neigh,
    w2_self,
    w2_neigh,
    send_rows,
    send_count,
    recv_target,
    out_grad,
):
    dma = pltpu.SemaphoreType.DMA
    hbm = pl.BlockSpec(memory_space=pl.ANY)
    layer_out, grad_self, grad_neigh = pl.pallas_call(
        kernel,
        out_shape=(
            jax.ShapeDtypeStruct((16, 512), BF16),
            jax.ShapeDtypeStruct((16, 512), F32),
            jax.ShapeDtypeStruct((16, 512), F32),
        ),
        in_specs=[hbm] * 10,
        out_specs=(hbm, hbm, hbm),
        scratch_shapes=[
            pltpu.VMEM((16, 2048), BF16),
            pltpu.VMEM((K1, 1, 1024), jnp.int32),
            pltpu.VMEM((16, 512), BF16),
            pltpu.VMEM((16, 512), BF16),
            pltpu.VMEM((512, 512), BF16),
            pltpu.VMEM((512, 512), BF16),
            pltpu.VMEM((8, 16), jnp.int32),
            pltpu.VMEM((1, 16), jnp.int32),
            pltpu.VMEM((8, 16), jnp.int32),
            pltpu.VMEM((16, 512), BF16),
            pltpu.VMEM((16, 512), BF16),
            pltpu.VMEM((16, 512), F32),
            pltpu.VMEM((16, 512), F32),
            pltpu.VMEM((GROUPS, 2, 16, LANES), BF16),
            pltpu.VMEM((GROUPS, 2, 16, LANES), BF16),
            pltpu.VMEM((NZ, 16, LANES), BF16),
            pltpu.VMEM((NZ, 16, LANES), BF16),
            pltpu.VMEM((8, 16, LANES), BF16),
            pltpu.VMEM((7, 16, LANES), BF16),
            pltpu.VMEM((NDP, 256, LANES), BF16),
            pltpu.VMEM((16, LANES), BF16),
            pltpu.VMEM((16, LANES), BF16),
            pltpu.VMEM((NDP, 8, LANES), F32),
            pltpu.VMEM((NDP, 16, 512), BF16),
            pltpu.VMEM((NDP, 16, 512), BF16),
            pltpu.VMEM((16, 512), BF16),
            pltpu.VMEM((16, 512), BF16),
            pltpu.VMEM((16, 512), BF16),
            pltpu.VMEM((16, 2, 16, 512), BF16),
            pltpu.VMEM((2, 32, 512), F32),
            pltpu.VMEM((32, 512), F32),
            pltpu.VMEM((64, 512), F32),
            pltpu.VMEM((32, 512), F32),
            dma((13,)),
            dma((NZ,)),
            dma((NZ,)),
            dma((2,)),
            dma((2,)),
            dma((16,)),
            dma((16,)),
            dma((2,)),
            dma((1,)),
            dma((NDP,)),
            dma((NDP,)),
            dma((NDP,)),
            dma((NDP,)),
            dma((NDP,)),
            dma((NDP,)),
            dma((NDP,)),
            dma((NDP,)),
            dma((2,)),
            dma((2,)),
            dma((16,)),
            dma((16,)),
            dma((3,)),
            dma((3,)),
        ],
        compiler_params=pltpu.CompilerParams(
            collective_id=0, has_side_effects=True, vmem_limit_bytes=64 * 1024 * 1024
        ),
    )(
        features[0],
        jnp.transpose(neigh_lists, (1, 0, 2)),
        w1_self,
        w1_neigh,
        w2_self,
        w2_neigh,
        jnp.transpose(send_rows[0, 0]),
        send_count[0],
        jnp.transpose(recv_target[0, 0]),
        out_grad[0, 0],
    )
    return layer_out[None, None], grad_self[None], grad_neigh[None]


def solution(mesh):
    in_specs = (
        P("dp", "feat", None),
        P("dp", None, None),
        P("feat", None),
        P("feat", None),
        P(),
        P(),
        P("dp", "feat", None, None),
        P("dp", "feat", None),
        P("dp", "feat", None, None),
        P("dp", "feat", None, None),
    )
    out_specs = (P("dp", "feat", None, None), P("dp", "feat", None), P("dp", "feat", None))
    return jax.shard_map(
        on_device, mesh=mesh, in_specs=in_specs, out_specs=out_specs, check_vma=False
    )
```

```python
import functools

import jax
import jax.numpy as jnp
from jax import lax
from jax.experimental import pallas as pl
from jax.experimental.pallas import tpu as pltpu
from jax.sharding import PartitionSpec as P

MESH = pl.DeviceIdType.MESH
K1 = 10
NZ = 32
NDP = 16
GROUPS = 8
LANES = 128
F32 = jnp.float32
BF16 = jnp.bfloat16

WINDOW_PLAN = (
    (0, (5, -5, -8, 2, -2, 1, -1)),
    (5, (2, -2, 1, -1)),
    (-5, (2, -2, 1, -1)),
)


def place(offset):
    if offset <= -16:
        offset += NZ
    if -7 <= offset <= 8:
        at = (offset + 7) // 2
    else:
        at = 8 + (offset - 9) // 2 if offset > 0 else 12 + (-offset - 8) // 2
    return offset % 2 * 16 + at


assert sorted(place(o) for o in range(-15, 17)) == list(range(NZ))


def iota(shape, axis):
    return lax.broadcasted_iota(jnp.int32, shape, axis)


def dot(a, b):
    return jnp.dot(a, b, preferred_element_type=F32)


def dot_nt(a, b):
    return lax.dot_general(a, b, (((1,), (1,)), ((), ())), preferred_element_type=F32)


def kernel(
    feat_in,
    lists_in,
    w1s_in,
    w1n_in,
    w2s_in,
    w2n_in,
    rows_in_hbm,
    count_in_hbm,
    target_in_hbm,
    og_in,
    out_hbm,
    gs_hbm,
    gn_hbm,
    feat_ref,
    lists_ref,
    w1s_ref,
    w1n_ref,
    w2s_ref,
    w2n_ref,
    rows_ref,
    count_ref,
    target_ref,
    og_ref,
    out_ref,
    gs_ref,
    gn_ref,
    xs,
    xp,
    tiles,
    slots,
    relay_up,
    relay_down,
    w,
    w_own,
    w_relay,
    meta,
    gm_all,
    h_all,
    gh_own,
    gh_opp,
    gp,
    part,
    part_in,
    res,
    res_in,
    local_s,
    x_s,
    x_r,
    relay_s,
    relay_r,
    wz_s,
    wz_r,
    wr_r,
    wd_s,
    wd_r,
    meta_s,
    meta_r,
    gm_s,
    gm_r,
    h_s,
    h_r,
    gh_s,
    gh_r,
    hello,
    gp_s,
    gp_r,
    d2d_s,
    d2d_r,
):
    f = lax.axis_index("feat")
    d = lax.axis_index("dp")
    z = f // 2
    q = lax.rem(f, 2)
    partner = {"feat": 2 * z + 1 - q}
    sends = []

    def chip(offset):
        return {"feat": 2 * lax.rem(z + offset + NZ, NZ) + q}

    def row_peer(i):
        return lax.rem(d + i, NDP)

    def copy(src, dst, send, recv, device):
        return pltpu.make_async_remote_copy(
            src_ref=src, dst_ref=dst, send_sem=send, recv_sem=recv, device_id=device, device_id_type=MESH
        )

    def send(src, dst, send_sem, recv_sem, device):
        c = copy(src, dst, send_sem, recv_sem, device)
        c.start()
        sends.append(c)
        return c

    def arrived(dst, recv_sem):
        copy(dst, dst, d2d_s.at[0], recv_sem, partner).wait_recv()

    def to_row(src, dst, send_sem, recv_sem):
        @pl.loop(1, NDP)
        def _(i):
            copy(src, dst, send_sem.at[i], recv_sem.at[d], {"dp": row_peer(i)}).start()

    def from_row(buf, recv_sem):
        @pl.loop(1, NDP)
        def _(i):
            e = row_peer(i)
            arrived(buf.at[e], recv_sem.at[e])

    pairs = (
        (feat_in, feat_ref),
        (lists_in, lists_ref),
        (rows_in_hbm, rows_ref),
        (count_in_hbm, count_ref),
        (target_in_hbm, target_ref),
        (w1s_in, w1s_ref),
        (w1n_in, w1n_ref),
        (og_in, og_ref),
        (w2n_in, w2n_ref),
        (w2s_in, w2s_ref),
    )
    loads = [pltpu.make_async_copy(src, dst, local_s.at[n]) for n, (src, dst) in enumerate(pairs)]
    for c in loads[:2]:
        c.start()

    barrier = pltpu.get_barrier_semaphore()

    def signal(device):
        pl.semaphore_signal(barrier, inc=1, device_id=device, device_id_type=MESH)

    for offset in range(8, 0, -1):
        signal(chip(offset))
        signal(chip(-offset))
    signal(partner)

    @pl.loop(1, NDP)
    def _(i):
        signal({"dp": row_peer(i)})

    for c in loads[2:]:
        c.start()
    for c in loads[:2]:
        c.wait()

    chunks = [feat_ref[:, LANES * i : LANES * (i + 1)].astype(F32) for i in range(16)]

    @pl.loop(0, GROUPS)
    def _(c):
        lanes = pl.ds(pl.multiple_of(c * LANES, LANES), LANES)
        total = jnp.zeros((16, LANES), F32)
        for k in range(K1):
            index = jnp.broadcast_to(lists_ref[k, :, lanes], (16, LANES))
            low = lax.bitwise_and(index, 127)
            high = lax.shift_right_logical(index, 7)
            value = jnp.zeros((16, LANES), F32)
            for i in range(16):
                picked = jnp.take_along_axis(chunks[i], low, axis=1, mode="promise_in_bounds")
                value = jnp.where(high == i, picked, value)
            total += value
        xs[c, 0] = feat_ref[:, lanes]
        xs[c, 1] = (total / K1).astype(BF16)

    quarter = iota((16, LANES), 1) // 32

    @pl.loop(0, GROUPS)
    def _(c):
        far = lax.rem(c + 4, GROUPS)
        parts = [xs[c, 0], xs[c, 1], xs[far, 0], xs[far, 1]]
        parts = [p.astype(F32) for p in parts]
        for i in range(4):
            tile = jnp.zeros((16, LANES), F32)
            for k in range(4):
                shift = (32 * (k - i)) % LANES
                moved = pltpu.roll(parts[k], shift, 1) if shift else parts[k]
                tile = jnp.where(quarter == k, moved, tile)
            tiles[lax.rem(4 * c + i - z + NZ, NZ)] = tile.astype(BF16)

    slots[place(0)] = tiles[0]

    lane = iota((1, LANES), 1)
    slot = lax.rem(lane, 8)
    peer_rows = iota((NDP, LANES), 0) == iota((NDP, LANES), 1) // 8
    spread = peer_rows.astype(F32).astype(BF16)
    own_slot = iota((8, LANES), 0) == lax.rem(iota((8, LANES), 1), 8)

    for c in loads[2:7]:
        c.wait()

    def flat(ref):
        wide = dot(ref[...].astype(F32).astype(BF16), spread)
        return jnp.sum(jnp.where(own_slot, wide, 0.0), axis=0, keepdims=True)

    rows_own = flat(rows_ref)
    target_own = flat(target_ref)
    count_own = dot(count_ref[...].astype(F32).astype(BF16), spread)
    meta[d] = jnp.concatenate([rows_own, target_own, count_own, jnp.zeros((5, LANES), F32)], axis=0)

    piece = lax.rem(d, 8)
    w_lanes = pl.ds(pl.multiple_of(lax.rem(d, 4) * LANES, LANES), LANES)
    parity = d // 8
    own_tile = jnp.where(piece < 4, w1s_ref[:, w_lanes].astype(F32), w1n_ref[:, w_lanes].astype(F32)).astype(BF16)
    w_own[...] = own_tile

    @pl.when(parity == 0)
    def _():
        w[d, pl.ds(16 * place(0), 16), :] = own_tile

    def w_at(offset):
        return w.at[d, pl.ds(16 * (place(offset) % 16), 16), :]

    pl.semaphore_wait(barrier, 16 + 1 + NDP - 1)

    send(tiles.at[pl.ds(9, 8)], relay_up, relay_s.at[0], relay_r.at[0], chip(8))
    send(tiles.at[pl.ds(17, 7)], relay_down, relay_s.at[1], relay_r.at[1], chip(-8))

    w_direct, w_passed, w_near, w_far = [], [], [], []
    for p in (0, 1):
        up, down = (w_at(-8), w_at(8)) if p == 0 else (w_relay.at[0], w_relay.at[1])
        up_sem, down_sem = (
            (wz_r.at[place(-8) % 16], wz_r.at[place(8) % 16]) if p == 0 else (wr_r.at[0], wr_r.at[1])
        )
        near = [t for k in range(7, 0, -1) for t in (k, -k) if k % 2 == p]
        direct = [(8, up, up_sem), (-8, down, down_sem)]
        direct += [(t, w_at(-t), wz_r.at[place(-t) % 16]) for t in near]
        w_direct.append([copy(w_own, dst, wz_s.at[n], sem, chip(t)) for n, (t, dst, sem) in enumerate(direct)])
        passed = [(up, -8 - t, t) for t in range(8, 0, -1) if t % 2 == p]
        passed += [(down, 8 + t, -t) for t in range(7, 0, -1) if t % 2 == p]
        w_passed.append(
            [
                copy(src, w_at(offset), wz_s.at[10 + n], wz_r.at[place(offset) % 16], chip(t))
                for n, (src, offset, t) in enumerate(passed)
            ]
        )
        w_near.append(near)
        w_far.append([offset + (NZ if offset == -16 else 0) for _, offset, _ in passed])

    def by_parity(body):
        for p in (0, 1):
            pl.when(parity == p)(functools.partial(body, p))

    def start_weights(p):
        for c in w_direct[p]:
            c.start()

    def pass_weights(p):
        if p == 0:
            arrived(w_at(-8), wz_r.at[place(-8) % 16])
            arrived(w_at(8), wz_r.at[place(8) % 16])
        else:
            arrived(w_relay.at[0], wr_r.at[0])
            arrived(w_relay.at[1], wr_r.at[1])
        for c in w_passed[p]:
            c.start()
        for t in w_near[p]:
            arrived(w_at(-t), wz_r.at[place(-t) % 16])

    def far_weights(p):
        for offset in w_far[p]:
            arrived(w_at(offset), wz_r.at[place(offset) % 16])

    def sent_weights(p):
        for c in w_direct[p] + w_passed[p]:
            c.wait_send()

    by_parity(start_weights)

    for k in range(8, 0, -1):
        for t in (k, -k):
            send(tiles.at[t % NZ], slots.at[place(-t)], x_s.at[t + 8], x_r.at[place(-t)], chip(t))

    to_row(meta.at[d], meta.at[d], meta_s, meta_r)

    loads[7].wait()
    loads[8].wait()
    og = og_ref[...]
    raw_mean = dot_nt(og, w2n_ref[...])
    gm_all[d] = raw_mean.astype(BF16)
    to_row(gm_all.at[d], gm_all.at[d], gm_s, gm_r)
    pl.semaphore_signal(hello, inc=1, device_id=chip(8), device_id_type=MESH)
    send(xs, xp, d2d_s.at[0], d2d_r.at[0], partner)
    loads[9].wait()
    grad_self = dot_nt(og, w2s_ref[...])

    from_row(meta, meta_r)
    mine = iota((NDP, LANES), 1) // 8 == d
    same_slot = (lax.rem(iota((LANES, LANES), 0), 8) == lax.rem(iota((LANES, LANES), 1), 8)).astype(BF16)

    def from_peers(row):
        wide = dot(jnp.where(mine, meta[:, row, :], 0.0).astype(BF16), same_slot)
        return jnp.sum(jnp.where(peer_rows, wide, 0.0), axis=0, keepdims=True)

    rows_in = from_peers(0)
    target_in = from_peers(1)
    count_in = from_peers(2)
    slot_f = slot.astype(F32)
    base = (lane // 8 * 16).astype(F32)
    node = iota((16, LANES), 0).astype(F32)
    hits_in = jnp.where((target_own == node) & (slot_f < count_in), 1.0, 0.0)
    degree = jnp.sum(hits_in, axis=1, keepdims=True)

    hits_out = jnp.where((rows_own == node) & (slot_f < count_own), 1.0, 0.0)
    everyone = iota((NDP * 16, LANES), 0).astype(F32)
    table_in = jnp.where(everyone == base + rows_in, 1.0, 0.0).astype(BF16)
    table_out = jnp.where(everyone == base + target_in, 1.0, 0.0).astype(BF16)
    mix_in = dot_nt(hits_in.astype(BF16), table_in).astype(BF16)
    mix_out = dot_nt(hits_out.astype(BF16), table_out).astype(BF16)

    first_lane = (iota((NDP, LANES), 1) == 8 * iota((NDP, LANES), 0)).astype(F32).astype(BF16)
    count_to = dot_nt(first_lane, meta[:, 2, :].astype(BF16)).astype(BF16)
    live = lax.rem(iota((NDP, LANES), 1), 8).astype(F32) < dot(count_to, spread)
    aims = jnp.where(live, meta[:, 1, :], 31.0).astype(BF16)
    repeat = (iota((NDP * 16, NDP), 0) // 16 == iota((NDP * 16, NDP), 1)).astype(F32).astype(BF16)
    hits = dot(repeat, aims) == lax.rem(iota((NDP * 16, LANES), 0), 16).astype(F32)
    degrees = jnp.sum(jnp.where(hits, 1.0, 0.0), axis=1, keepdims=True)

    from_row(gm_all, gm_r)
    returned = gm_all[...].reshape(NDP * 16, 512).astype(F32) / (1.0 + degrees)
    back = jnp.dot(mix_out.astype(F32), returned, precision=lax.Precision.HIGHEST, preferred_element_type=F32)
    gh_own[...] = (grad_self + raw_mean / (1.0 + degree) + back).astype(BF16)
    pl.semaphore_wait(hello, 1)
    send(gh_own, gh_opp, gh_s.at[0], gh_r.at[0], chip(16))

    arrived(relay_up, relay_r.at[0])
    for t in range(8, 0, -1):
        send(relay_up.at[t - 1], slots.at[place(-8 - t)], x_s.at[16 + t], x_r.at[place(-8 - t)], chip(t))
    arrived(relay_down, relay_r.at[1])
    for t in range(7, 0, -1):
        send(relay_down.at[7 - t], slots.at[place(8 + t)], x_s.at[24 + t], x_r.at[place(8 + t)], chip(-t))

    by_parity(pass_weights)
    early = pl.ds(0, 128)
    late = pl.ds(128, 128)
    to_row(w.at[d, early], w.at[d, early], wd_s.at[0], wd_r.at[0])

    arrived(xp, d2d_r.at[0])
    node_in = iota((1024, 512), 0)
    node_at = iota((1024, 512), 1)
    block_at = node_at // 16
    chip_at = lax.rem(z - 7 + NZ + block_at // 2 + 16 * lax.rem(block_at, 2), NZ)
    pick = jnp.where(node_in == 32 * chip_at + 16 * q + lax.rem(node_at, 16), 1.0, 0.0).astype(BF16)
    wide_rows = jnp.concatenate(
        [
            jnp.concatenate([buf[c, kind] for c in range(GROUPS)], axis=1)
            for buf in (xs, xp)
            for kind in (0, 1)
        ],
        axis=0,
    )
    x_cols = dot(wide_rows, pick).astype(BF16)

    by_parity(far_weights)
    to_row(w.at[d, late], w.at[d, late], wd_s.at[1], wd_r.at[1])

    for offset in range(-15, 17):
        if offset:
            arrived(slots.at[place(offset)], x_r.at[place(offset)])
    turned = [
        jnp.transpose(slots[16 * half : 16 * half + 16].reshape(256, LANES).astype(F32)).astype(BF16)
        for half in (0, 1)
    ]

    def rows_of(half, kind):
        t = turned[half]
        return jnp.concatenate([t[32 * kind : 32 * kind + 32], t[64 + 32 * kind : 96 + 32 * kind]], axis=0)

    x_rows = [[rows_of(half, kind) for kind in (0, 1)] for half in (0, 1)]

    @pl.loop(1, NDP)
    def _(i):
        e = row_peer(i)
        arrived(w.at[e, early], wd_r.at[0, e])
        arrived(w.at[e, late], wd_r.at[1, e])

    for block in range(4):
        total = jnp.zeros((64, LANES), F32)
        for half in (0, 1):
            for kind in (0, 1):
                total += dot(x_rows[half][kind], w[half * 8 + kind * 4 + block])
        lanes = slice(LANES * block, LANES * (block + 1))
        for core in (0, 1):
            part[core, 0:16, lanes] = total[16 * core : 16 * core + 16]
            part[core, 16:32, lanes] = total[32 + 16 * core : 48 + 16 * core]

    send(part.at[1 - q], part_in, d2d_s.at[1], d2d_r.at[1], partner)
    arrived(part_in, d2d_r.at[1])
    preact = part[q] + part_in[...]
    hidden = jnp.maximum(preact[0:16], 0.0).astype(BF16)
    arrived(gh_opp, gh_r.at[0])
    gp[7, 0] = jnp.where(preact[0:16] > 0, gh_own[...].astype(F32), 0.0).astype(BF16)
    gp[7, 1] = jnp.where(preact[16:32] > 0, gh_opp[...].astype(F32), 0.0).astype(BF16)
    h_all[d] = hidden

    def pass_on(offset, targets):
        for target in targets:
            there = offset - target + 7
            send(gp.at[offset + 7], gp.at[there], gp_s.at[there], gp_r.at[there], chip(target))

    pass_on(*WINDOW_PLAN[0])
    to_row(h_all.at[d], h_all.at[d], h_s, h_r)
    for offset, targets in WINDOW_PLAN[1:]:
        arrived(gp.at[offset + 7], gp_r.at[offset + 7])
        pass_on(offset, targets)

    from_row(h_all, h_r)
    stores = [
        pltpu.make_async_copy(src, dst, local_s.at[10 + n])
        for n, (src, dst) in enumerate(((out_ref, out_hbm), (gs_ref, gs_hbm), (gn_ref, gn_hbm)))
    ]
    neigh_sum = dot(mix_in, h_all[...].reshape(NDP * 16, 512))
    mean_two = ((hidden.astype(F32) + neigh_sum) / (1.0 + degree)).astype(BF16)
    out_ref[...] = (dot(hidden, w2s_ref[...]) + dot(mean_two, w2n_ref[...])).astype(BF16)
    stores[0].start()

    for offset in range(-7, 9):
        if offset not in (0, 5, -5):
            arrived(gp.at[offset + 7], gp_r.at[offset + 7])

    res[...] = dot(x_cols, gp[...].reshape(512, 512))
    send(res.at[32:64], res_in, d2d_s.at[2], d2d_r.at[2], partner)
    arrived(res_in, d2d_r.at[2])
    gs_ref[...] = res[0:16] + res_in[0:16]
    gn_ref[...] = res[16:32] + res_in[16:32]

    stores[1].start()
    stores[2].start()

    for c in sends:
        c.wait_send()

    by_parity(sent_weights)

    @pl.loop(1, NDP)
    def _(i):
        to = {"dp": row_peer(i)}
        copy(meta.at[d], meta.at[d], meta_s.at[i], meta_r.at[d], to).wait_send()
        copy(gm_all.at[d], gm_all.at[d], gm_s.at[i], gm_r.at[d], to).wait_send()
        copy(h_all.at[d], h_all.at[d], h_s.at[i], h_r.at[d], to).wait_send()
        copy(w.at[d, early], w.at[d, early], wd_s.at[0, i], wd_r.at[0, d], to).wait_send()
        copy(w.at[d, late], w.at[d, late], wd_s.at[1, i], wd_r.at[1, d], to).wait_send()

    for c in stores:
        c.wait()


def on_device(
    features,
    neigh_lists,
    w1_self,
    w1_neigh,
    w2_self,
    w2_neigh,
    send_rows,
    send_count,
    recv_target,
    out_grad,
):
    dma = pltpu.SemaphoreType.DMA
    hbm = pl.BlockSpec(memory_space=pl.ANY)
    layer_out, grad_self, grad_neigh = pl.pallas_call(
        kernel,
        out_shape=(
            jax.ShapeDtypeStruct((16, 512), BF16),
            jax.ShapeDtypeStruct((16, 512), F32),
            jax.ShapeDtypeStruct((16, 512), F32),
        ),
        in_specs=[hbm] * 10,
        out_specs=(hbm, hbm, hbm),
        scratch_shapes=[
            pltpu.VMEM((16, 2048), BF16),
            pltpu.VMEM((K1, 1, 1024), jnp.int32),
            pltpu.VMEM((16, 512), BF16),
            pltpu.VMEM((16, 512), BF16),
            pltpu.VMEM((512, 512), BF16),
            pltpu.VMEM((512, 512), BF16),
            pltpu.VMEM((8, 16), jnp.int32),
            pltpu.VMEM((1, 16), jnp.int32),
            pltpu.VMEM((8, 16), jnp.int32),
            pltpu.VMEM((16, 512), BF16),
            pltpu.VMEM((16, 512), BF16),
            pltpu.VMEM((16, 512), F32),
            pltpu.VMEM((16, 512), F32),
            pltpu.VMEM((GROUPS, 2, 16, LANES), BF16),
            pltpu.VMEM((GROUPS, 2, 16, LANES), BF16),
            pltpu.VMEM((NZ, 16, LANES), BF16),
            pltpu.VMEM((NZ, 16, LANES), BF16),
            pltpu.VMEM((8, 16, LANES), BF16),
            pltpu.VMEM((7, 16, LANES), BF16),
            pltpu.VMEM((NDP, 256, LANES), BF16),
            pltpu.VMEM((16, LANES), BF16),
            pltpu.VMEM((2, 16, LANES), BF16),
            pltpu.VMEM((NDP, 8, LANES), F32),
            pltpu.VMEM((NDP, 16, 512), BF16),
            pltpu.VMEM((NDP, 16, 512), BF16),
            pltpu.VMEM((16, 512), BF16),
            pltpu.VMEM((16, 512), BF16),
            pltpu.VMEM((16, 2, 16, 512), BF16),
            pltpu.VMEM((2, 32, 512), F32),
            pltpu.VMEM((32, 512), F32),
            pltpu.VMEM((64, 512), F32),
            pltpu.VMEM((32, 512), F32),
            dma((13,)),
            dma((NZ,)),
            dma((NZ,)),
            dma((2,)),
            dma((2,)),
            dma((18,)),
            dma((16,)),
            dma((2,)),
            dma((2, NDP)),
            dma((2, NDP)),
            dma((NDP,)),
            dma((NDP,)),
            dma((NDP,)),
            dma((NDP,)),
            dma((NDP,)),
            dma((NDP,)),
            dma((1,)),
            dma((1,)),
            pltpu.SemaphoreType.REGULAR,
            dma((16,)),
            dma((16,)),
            dma((3,)),
            dma((3,)),
        ],
        compiler_params=pltpu.CompilerParams(
            collective_id=0, has_side_effects=True, vmem_limit_bytes=64 * 1024 * 1024
        ),
    )(
        features[0],
        jnp.transpose(neigh_lists, (1, 0, 2)),
        w1_self,
        w1_neigh,
        w2_self,
        w2_neigh,
        jnp.transpose(send_rows[0, 0]),
        send_count[0],
        jnp.transpose(recv_target[0, 0]),
        out_grad[0, 0],
    )
    return layer_out[None, None], grad_self[None], grad_neigh[None]


def solution(mesh):
    in_specs = (
        P("dp", "feat", None),
        P("dp", None, None),
        P("feat", None),
        P("feat", None),
        P(),
        P(),
        P("dp", "feat", None, None),
        P("dp", "feat", None),
        P("dp", "feat", None, None),
        P("dp", "feat", None, None),
    )
    out_specs = (P("dp", "feat", None, None), P("dp", "feat", None), P("dp", "feat", None))
    return jax.shard_map(
        on_device, mesh=mesh, in_specs=in_specs, out_specs=out_specs, check_vma=False
    )
```

```python
import functools

import jax
import jax.numpy as jnp
from jax import lax
from jax.experimental import pallas as pl
from jax.experimental.pallas import tpu as pltpu
from jax.sharding import PartitionSpec as P

MESH = pl.DeviceIdType.MESH
K1 = 10
NZ = 32
NDP = 16
GROUPS = 8
LANES = 128
F32 = jnp.float32
BF16 = jnp.bfloat16

WINDOW_PLAN = (
    (0, (5, -5, -8, 2, -2, 1, -1)),
    (5, (2, -2, 1, -1)),
    (-5, (2, -2, 1, -1)),
)


def place(offset):
    if offset <= -16:
        offset += NZ
    if -7 <= offset <= 8:
        at = (offset + 7) // 2
    else:
        step = (offset - 9) // 2 if offset > 0 else (-offset - 8) // 2
        at = 8 + 4 * (step // 2) + step % 2 + (0 if offset > 0 else 2)
    return offset % 2 * 16 + at


assert sorted(place(o) for o in range(-15, 17)) == list(range(NZ))


def iota(shape, axis):
    return lax.broadcasted_iota(jnp.int32, shape, axis)


def dot(a, b):
    return jnp.dot(a, b, preferred_element_type=F32)


def dot_nt(a, b):
    return lax.dot_general(a, b, (((1,), (1,)), ((), ())), preferred_element_type=F32)


def kernel(
    feat_in,
    lists_in,
    w1s_in,
    w1n_in,
    w2s_in,
    w2n_in,
    rows_in_hbm,
    count_in_hbm,
    target_in_hbm,
    og_in,
    out_hbm,
    gs_hbm,
    gn_hbm,
    feat_ref,
    lists_ref,
    w1s_ref,
    w1n_ref,
    w2s_ref,
    w2n_ref,
    rows_ref,
    count_ref,
    target_ref,
    og_ref,
    out_ref,
    gs_ref,
    gn_ref,
    xs,
    xp,
    tiles,
    slots,
    relay_up,
    relay_down,
    w,
    w_own,
    w_relay,
    meta,
    gm_all,
    h_all,
    gh_own,
    gh_opp,
    gp,
    part,
    part_in,
    res,
    res_in,
    local_s,
    x_s,
    x_r,
    relay_s,
    relay_r,
    wz_s,
    wz_r,
    wr_r,
    wd_s,
    wd_r,
    meta_s,
    meta_r,
    gm_s,
    gm_r,
    h_s,
    h_r,
    gh_s,
    gh_r,
    hello,
    gp_s,
    gp_r,
    d2d_s,
    d2d_r,
):
    f = lax.axis_index("feat")
    d = lax.axis_index("dp")
    z = f // 2
    q = lax.rem(f, 2)
    partner = {"feat": 2 * z + 1 - q}
    sends = []

    def chip(offset):
        return {"feat": 2 * lax.rem(z + offset + NZ, NZ) + q}

    def row_peer(i):
        return lax.rem(d + i, NDP)

    def copy(src, dst, send, recv, device):
        return pltpu.make_async_remote_copy(
            src_ref=src, dst_ref=dst, send_sem=send, recv_sem=recv, device_id=device, device_id_type=MESH
        )

    def send(src, dst, send_sem, recv_sem, device):
        c = copy(src, dst, send_sem, recv_sem, device)
        c.start()
        sends.append(c)
        return c

    def arrived(dst, recv_sem):
        copy(dst, dst, d2d_s.at[0], recv_sem, partner).wait_recv()

    def to_row(src, dst, send_sem, recv_sem):
        @pl.loop(1, NDP)
        def _(i):
            copy(src, dst, send_sem.at[i], recv_sem.at[d], {"dp": row_peer(i)}).start()

    def from_row(buf, recv_sem):
        @pl.loop(1, NDP)
        def _(i):
            e = row_peer(i)
            arrived(buf.at[e], recv_sem.at[e])

    pairs = (
        (feat_in, feat_ref),
        (lists_in, lists_ref),
        (rows_in_hbm, rows_ref),
        (count_in_hbm, count_ref),
        (target_in_hbm, target_ref),
        (w1s_in, w1s_ref),
        (w1n_in, w1n_ref),
        (og_in, og_ref),
        (w2n_in, w2n_ref),
        (w2s_in, w2s_ref),
    )
    loads = [pltpu.make_async_copy(src, dst, local_s.at[n]) for n, (src, dst) in enumerate(pairs)]
    for c in loads[:2]:
        c.start()

    barrier = pltpu.get_barrier_semaphore()

    def signal(device):
        pl.semaphore_signal(barrier, inc=1, device_id=device, device_id_type=MESH)

    for offset in range(8, 0, -1):
        signal(chip(offset))
        signal(chip(-offset))
    signal(partner)

    @pl.loop(1, NDP)
    def _(i):
        signal({"dp": row_peer(i)})

    for c in loads[2:]:
        c.start()
    for c in loads[:2]:
        c.wait()

    chunks = [feat_ref[:, LANES * i : LANES * (i + 1)].astype(F32) for i in range(16)]

    @pl.loop(0, GROUPS)
    def _(c):
        lanes = pl.ds(pl.multiple_of(c * LANES, LANES), LANES)
        total = jnp.zeros((16, LANES), F32)
        for k in range(K1):
            index = jnp.broadcast_to(lists_ref[k, :, lanes], (16, LANES))
            low = lax.bitwise_and(index, 127)
            high = lax.shift_right_logical(index, 7)
            value = jnp.zeros((16, LANES), F32)
            for i in range(16):
                picked = jnp.take_along_axis(chunks[i], low, axis=1, mode="promise_in_bounds")
                value = jnp.where(high == i, picked, value)
            total += value
        xs[c, 0] = feat_ref[:, lanes]
        xs[c, 1] = (total / K1).astype(BF16)

    quarter = iota((16, LANES), 1) // 32

    @pl.loop(0, GROUPS)
    def _(c):
        far = lax.rem(c + 4, GROUPS)
        parts = [xs[c, 0], xs[c, 1], xs[far, 0], xs[far, 1]]
        parts = [p.astype(F32) for p in parts]
        for i in range(4):
            tile = jnp.zeros((16, LANES), F32)
            for k in range(4):
                shift = (32 * (k - i)) % LANES
                moved = pltpu.roll(parts[k], shift, 1) if shift else parts[k]
                tile = jnp.where(quarter == k, moved, tile)
            tiles[lax.rem(4 * c + i - z + NZ, NZ)] = tile.astype(BF16)

    slots[place(0)] = tiles[0]

    lane = iota((1, LANES), 1)
    slot = lax.rem(lane, 8)
    peer_rows = iota((NDP, LANES), 0) == iota((NDP, LANES), 1) // 8
    spread = peer_rows.astype(F32).astype(BF16)
    own_slot = iota((8, LANES), 0) == lax.rem(iota((8, LANES), 1), 8)

    for c in loads[2:7]:
        c.wait()

    def flat(ref):
        wide = dot(ref[...].astype(F32).astype(BF16), spread)
        return jnp.sum(jnp.where(own_slot, wide, 0.0), axis=0, keepdims=True)

    rows_own = flat(rows_ref)
    target_own = flat(target_ref)
    count_own = dot(count_ref[...].astype(F32).astype(BF16), spread)
    meta[d] = jnp.concatenate([rows_own, target_own, count_own, jnp.zeros((5, LANES), F32)], axis=0)

    piece = lax.rem(d, 8)
    w_lanes = pl.ds(pl.multiple_of(lax.rem(d, 4) * LANES, LANES), LANES)
    parity = d // 8
    own_tile = jnp.where(piece < 4, w1s_ref[:, w_lanes].astype(F32), w1n_ref[:, w_lanes].astype(F32)).astype(BF16)
    w_own[...] = own_tile

    @pl.when(parity == 0)
    def _():
        w[d, pl.ds(16 * place(0), 16), :] = own_tile

    def w_at(offset):
        return w.at[d, pl.ds(16 * (place(offset) % 16), 16), :]

    pl.semaphore_wait(barrier, 16 + 1 + NDP - 1)

    send(tiles.at[pl.ds(9, 8)], relay_up, relay_s.at[0], relay_r.at[0], chip(8))
    send(tiles.at[pl.ds(17, 7)], relay_down, relay_s.at[1], relay_r.at[1], chip(-8))

    w_direct, w_passed, w_near, w_far = [], [], [], []
    for p in (0, 1):
        up, down = (w_at(-8), w_at(8)) if p == 0 else (w_relay.at[0], w_relay.at[1])
        up_sem, down_sem = (
            (wz_r.at[place(-8) % 16], wz_r.at[place(8) % 16]) if p == 0 else (wr_r.at[0], wr_r.at[1])
        )
        near = [t for k in range(7, 0, -1) for t in (k, -k) if k % 2 == p]
        direct = [(8, up, up_sem), (-8, down, down_sem)]
        direct += [(t, w_at(-t), wz_r.at[place(-t) % 16]) for t in near]
        w_direct.append([copy(w_own, dst, wz_s.at[n], sem, chip(t)) for n, (t, dst, sem) in enumerate(direct)])
        passed = [(up, -8 - t, t) for t in range(8, 0, -1) if t % 2 == p]
        passed += [(down, 8 + t, -t) for t in range(7, 0, -1) if t % 2 == p]
        w_passed.append(
            [
                copy(src, w_at(offset), wz_s.at[10 + n], wz_r.at[place(offset) % 16], chip(t))
                for n, (src, offset, t) in enumerate(passed)
            ]
        )
        w_near.append(near)
        w_far.append([offset + (NZ if offset == -16 else 0) for _, offset, _ in passed])

    def by_parity(body):
        for p in (0, 1):
            pl.when(parity == p)(functools.partial(body, p))

    def start_weights(p):
        for c in w_direct[p]:
            c.start()

    def pass_weights(p):
        if p == 0:
            arrived(w_at(-8), wz_r.at[place(-8) % 16])
            arrived(w_at(8), wz_r.at[place(8) % 16])
        else:
            arrived(w_relay.at[0], wr_r.at[0])
            arrived(w_relay.at[1], wr_r.at[1])
        for c in w_passed[p]:
            c.start()
        for t in w_near[p]:
            arrived(w_at(-t), wz_r.at[place(-t) % 16])

    def far_weights(p, first):
        for offset in w_far[p]:
            if (place(offset) % 16 < 12) == first:
                arrived(w_at(offset), wz_r.at[place(offset) % 16])

    def sent_weights(p):
        for c in w_direct[p] + w_passed[p]:
            c.wait_send()

    by_parity(start_weights)

    for k in range(8, 0, -1):
        for t in (k, -k):
            send(tiles.at[t % NZ], slots.at[place(-t)], x_s.at[t + 8], x_r.at[place(-t)], chip(t))

    to_row(meta.at[d], meta.at[d], meta_s, meta_r)

    loads[7].wait()
    loads[8].wait()
    og = og_ref[...]
    raw_mean = dot_nt(og, w2n_ref[...])
    gm_all[d] = raw_mean.astype(BF16)
    to_row(gm_all.at[d], gm_all.at[d], gm_s, gm_r)
    pl.semaphore_signal(hello, inc=1, device_id=chip(8), device_id_type=MESH)
    send(xs, xp, d2d_s.at[0], d2d_r.at[0], partner)
    loads[9].wait()
    grad_self = dot_nt(og, w2s_ref[...])

    from_row(meta, meta_r)
    mine = iota((NDP, LANES), 1) // 8 == d
    same_slot = (lax.rem(iota((LANES, LANES), 0), 8) == lax.rem(iota((LANES, LANES), 1), 8)).astype(BF16)

    def from_peers(row):
        wide = dot(jnp.where(mine, meta[:, row, :], 0.0).astype(BF16), same_slot)
        return jnp.sum(jnp.where(peer_rows, wide, 0.0), axis=0, keepdims=True)

    rows_in = from_peers(0)
    target_in = from_peers(1)
    count_in = from_peers(2)
    slot_f = slot.astype(F32)
    base = (lane // 8 * 16).astype(F32)
    node = iota((16, LANES), 0).astype(F32)
    hits_in = jnp.where((target_own == node) & (slot_f < count_in), 1.0, 0.0)
    degree = jnp.sum(hits_in, axis=1, keepdims=True)

    hits_out = jnp.where((rows_own == node) & (slot_f < count_own), 1.0, 0.0)
    everyone = iota((NDP * 16, LANES), 0).astype(F32)
    table_in = jnp.where(everyone == base + rows_in, 1.0, 0.0).astype(BF16)
    table_out = jnp.where(everyone == base + target_in, 1.0, 0.0).astype(BF16)
    mix_in = dot_nt(hits_in.astype(BF16), table_in).astype(BF16)
    mix_out = dot_nt(hits_out.astype(BF16), table_out).astype(BF16)

    first_lane = (iota((NDP, LANES), 1) == 8 * iota((NDP, LANES), 0)).astype(F32).astype(BF16)
    count_to = dot_nt(first_lane, meta[:, 2, :].astype(BF16)).astype(BF16)
    live = lax.rem(iota((NDP, LANES), 1), 8).astype(F32) < dot(count_to, spread)
    aims = jnp.where(live, meta[:, 1, :], 31.0).astype(BF16)
    repeat = (iota((NDP * 16, NDP), 0) // 16 == iota((NDP * 16, NDP), 1)).astype(F32).astype(BF16)
    hits = dot(repeat, aims) == lax.rem(iota((NDP * 16, LANES), 0), 16).astype(F32)
    degrees = jnp.sum(jnp.where(hits, 1.0, 0.0), axis=1, keepdims=True)

    from_row(gm_all, gm_r)
    returned = gm_all[...].reshape(NDP * 16, 512).astype(F32) / (1.0 + degrees)
    back = jnp.dot(mix_out.astype(F32), returned, precision=lax.Precision.HIGHEST, preferred_element_type=F32)
    gh_own[...] = (grad_self + raw_mean / (1.0 + degree) + back).astype(BF16)
    pl.semaphore_wait(hello, 1)
    send(gh_own, gh_opp, gh_s.at[0], gh_r.at[0], chip(16))

    arrived(relay_up, relay_r.at[0])
    for t in range(8, 0, -1):
        send(relay_up.at[t - 1], slots.at[place(-8 - t)], x_s.at[16 + t], x_r.at[place(-8 - t)], chip(t))
    arrived(relay_down, relay_r.at[1])
    for t in range(7, 0, -1):
        send(relay_down.at[7 - t], slots.at[place(8 + t)], x_s.at[24 + t], x_r.at[place(8 + t)], chip(-t))

    by_parity(pass_weights)
    spans = (pl.ds(0, 128), pl.ds(128, 64), pl.ds(192, 64))

    def weights_to_row(n):
        to_row(w.at[d, spans[n]], w.at[d, spans[n]], wd_s.at[n], wd_r.at[n])

    def weights_from_row(n):
        @pl.loop(1, NDP)
        def _(i):
            e = row_peer(i)
            arrived(w.at[e, spans[n]], wd_r.at[n, e])

    weights_to_row(0)

    arrived(xp, d2d_r.at[0])
    node_in = iota((1024, 512), 0)
    node_at = iota((1024, 512), 1)
    block_at = node_at // 16
    chip_at = lax.rem(z - 7 + NZ + block_at // 2 + 16 * lax.rem(block_at, 2), NZ)
    pick = jnp.where(node_in == 32 * chip_at + 16 * q + lax.rem(node_at, 16), 1.0, 0.0).astype(BF16)
    wide_rows = jnp.concatenate(
        [
            jnp.concatenate([buf[c, kind] for c in range(GROUPS)], axis=1)
            for buf in (xs, xp)
            for kind in (0, 1)
        ],
        axis=0,
    )
    x_cols = dot(wide_rows, pick).astype(BF16)

    by_parity(functools.partial(far_weights, first=True))
    weights_to_row(1)
    by_parity(functools.partial(far_weights, first=False))
    weights_to_row(2)

    for offset in range(-15, 17):
        if offset:
            arrived(slots.at[place(offset)], x_r.at[place(offset)])
    turned = [
        jnp.transpose(slots[16 * half : 16 * half + 16].reshape(256, LANES).astype(F32)).astype(BF16)
        for half in (0, 1)
    ]

    def rows_of(half, kind):
        t = turned[half]
        return jnp.concatenate([t[32 * kind : 32 * kind + 32], t[64 + 32 * kind : 96 + 32 * kind]], axis=0)

    x_rows = [[rows_of(half, kind) for kind in (0, 1)] for half in (0, 1)]

    def products(block, k):
        total = jnp.zeros((64, LANES), F32)
        for half in (0, 1):
            for kind in (0, 1):
                total += dot(x_rows[half][kind][:, k], w[half * 8 + kind * 4 + block, k])
        return total

    weights_from_row(0)
    first_sums = [products(block, slice(0, 128)) for block in range(4)]
    weights_from_row(1)
    weights_from_row(2)
    for block in range(4):
        total = first_sums[block] + products(block, slice(128, 256))
        lanes = slice(LANES * block, LANES * (block + 1))
        for core in (0, 1):
            part[core, 0:16, lanes] = total[16 * core : 16 * core + 16]
            part[core, 16:32, lanes] = total[32 + 16 * core : 48 + 16 * core]

    send(part.at[1 - q], part_in, d2d_s.at[1], d2d_r.at[1], partner)
    arrived(part_in, d2d_r.at[1])
    preact = part[q] + part_in[...]
    hidden = jnp.maximum(preact[0:16], 0.0).astype(BF16)
    arrived(gh_opp, gh_r.at[0])
    gp[7, 0] = jnp.where(preact[0:16] > 0, gh_own[...].astype(F32), 0.0).astype(BF16)
    gp[7, 1] = jnp.where(preact[16:32] > 0, gh_opp[...].astype(F32), 0.0).astype(BF16)
    h_all[d] = hidden

    def pass_on(offset, targets):
        for target in targets:
            there = offset - target + 7
            send(gp.at[offset + 7], gp.at[there], gp_s.at[there], gp_r.at[there], chip(target))

    pass_on(*WINDOW_PLAN[0])
    to_row(h_all.at[d], h_all.at[d], h_s, h_r)
    for offset, targets in WINDOW_PLAN[1:]:
        arrived(gp.at[offset + 7], gp_r.at[offset + 7])
        pass_on(offset, targets)

    from_row(h_all, h_r)
    stores = [
        pltpu.make_async_copy(src, dst, local_s.at[10 + n])
        for n, (src, dst) in enumerate(((out_ref, out_hbm), (gs_ref, gs_hbm), (gn_ref, gn_hbm)))
    ]
    neigh_sum = dot(mix_in, h_all[...].reshape(NDP * 16, 512))
    mean_two = ((hidden.astype(F32) + neigh_sum) / (1.0 + degree)).astype(BF16)
    out_ref[...] = (dot(hidden, w2s_ref[...]) + dot(mean_two, w2n_ref[...])).astype(BF16)
    stores[0].start()

    for offset in range(-7, 9):
        if offset not in [o for o, _ in WINDOW_PLAN]:
            arrived(gp.at[offset + 7], gp_r.at[offset + 7])

    res[...] = dot(x_cols, gp[...].reshape(512, 512))
    send(res.at[32:64], res_in, d2d_s.at[2], d2d_r.at[2], partner)
    arrived(res_in, d2d_r.at[2])
    gs_ref[...] = res[0:16] + res_in[0:16]
    gn_ref[...] = res[16:32] + res_in[16:32]

    stores[1].start()
    stores[2].start()

    for c in sends:
        c.wait_send()

    by_parity(sent_weights)

    @pl.loop(1, NDP)
    def _(i):
        to = {"dp": row_peer(i)}
        copy(meta.at[d], meta.at[d], meta_s.at[i], meta_r.at[d], to).wait_send()
        copy(gm_all.at[d], gm_all.at[d], gm_s.at[i], gm_r.at[d], to).wait_send()
        copy(h_all.at[d], h_all.at[d], h_s.at[i], h_r.at[d], to).wait_send()
        for n in range(3):
            copy(w.at[d, spans[n]], w.at[d, spans[n]], wd_s.at[n, i], wd_r.at[n, d], to).wait_send()

    for c in stores:
        c.wait()


def on_device(
    features,
    neigh_lists,
    w1_self,
    w1_neigh,
    w2_self,
    w2_neigh,
    send_rows,
    send_count,
    recv_target,
    out_grad,
):
    dma = pltpu.SemaphoreType.DMA
    hbm = pl.BlockSpec(memory_space=pl.ANY)
    layer_out, grad_self, grad_neigh = pl.pallas_call(
        kernel,
        out_shape=(
            jax.ShapeDtypeStruct((16, 512), BF16),
            jax.ShapeDtypeStruct((16, 512), F32),
            jax.ShapeDtypeStruct((16, 512), F32),
        ),
        in_specs=[hbm] * 10,
        out_specs=(hbm, hbm, hbm),
        scratch_shapes=[
            pltpu.VMEM((16, 2048), BF16),
            pltpu.VMEM((K1, 1, 1024), jnp.int32),
            pltpu.VMEM((16, 512), BF16),
            pltpu.VMEM((16, 512), BF16),
            pltpu.VMEM((512, 512), BF16),
            pltpu.VMEM((512, 512), BF16),
            pltpu.VMEM((8, 16), jnp.int32),
            pltpu.VMEM((1, 16), jnp.int32),
            pltpu.VMEM((8, 16), jnp.int32),
            pltpu.VMEM((16, 512), BF16),
            pltpu.VMEM((16, 512), BF16),
            pltpu.VMEM((16, 512), F32),
            pltpu.VMEM((16, 512), F32),
            pltpu.VMEM((GROUPS, 2, 16, LANES), BF16),
            pltpu.VMEM((GROUPS, 2, 16, LANES), BF16),
            pltpu.VMEM((NZ, 16, LANES), BF16),
            pltpu.VMEM((NZ, 16, LANES), BF16),
            pltpu.VMEM((8, 16, LANES), BF16),
            pltpu.VMEM((7, 16, LANES), BF16),
            pltpu.VMEM((NDP, 256, LANES), BF16),
            pltpu.VMEM((16, LANES), BF16),
            pltpu.VMEM((2, 16, LANES), BF16),
            pltpu.VMEM((NDP, 8, LANES), F32),
            pltpu.VMEM((NDP, 16, 512), BF16),
            pltpu.VMEM((NDP, 16, 512), BF16),
            pltpu.VMEM((16, 512), BF16),
            pltpu.VMEM((16, 512), BF16),
            pltpu.VMEM((16, 2, 16, 512), BF16),
            pltpu.VMEM((2, 32, 512), F32),
            pltpu.VMEM((32, 512), F32),
            pltpu.VMEM((64, 512), F32),
            pltpu.VMEM((32, 512), F32),
            dma((13,)),
            dma((NZ,)),
            dma((NZ,)),
            dma((2,)),
            dma((2,)),
            dma((18,)),
            dma((16,)),
            dma((2,)),
            dma((3, NDP)),
            dma((3, NDP)),
            dma((NDP,)),
            dma((NDP,)),
            dma((NDP,)),
            dma((NDP,)),
            dma((NDP,)),
            dma((NDP,)),
            dma((1,)),
            dma((1,)),
            pltpu.SemaphoreType.REGULAR,
            dma((16,)),
            dma((16,)),
            dma((3,)),
            dma((3,)),
        ],
        compiler_params=pltpu.CompilerParams(
            collective_id=0, has_side_effects=True, vmem_limit_bytes=64 * 1024 * 1024
        ),
    )(
        features[0],
        jnp.transpose(neigh_lists, (1, 0, 2)),
        w1_self,
        w1_neigh,
        w2_self,
        w2_neigh,
        jnp.transpose(send_rows[0, 0]),
        send_count[0],
        jnp.transpose(recv_target[0, 0]),
        out_grad[0, 0],
    )
    return layer_out[None, None], grad_self[None], grad_neigh[None]


def solution(mesh):
    in_specs = (
        P("dp", "feat", None),
        P("dp", None, None),
        P("feat", None),
        P("feat", None),
        P(),
        P(),
        P("dp", "feat", None, None),
        P("dp", "feat", None),
        P("dp", "feat", None, None),
        P("dp", "feat", None, None),
    )
    out_specs = (P("dp", "feat", None, None), P("dp", "feat", None), P("dp", "feat", None))
    return jax.shard_map(
        on_device, mesh=mesh, in_specs=in_specs, out_specs=out_specs, check_vma=False
    )
```

```python
import functools

import jax
import jax.numpy as jnp
from jax import lax
from jax.experimental import pallas as pl
from jax.experimental.pallas import tpu as pltpu
from jax.sharding import PartitionSpec as P

MESH = pl.DeviceIdType.MESH
K1 = 10
NZ = 32
NDP = 16
GROUPS = 8
LANES = 128
F32 = jnp.float32
BF16 = jnp.bfloat16

WINDOW_PLAN = (
    (0, (3, -3, 1, -1)),
    (3, (-3, 1, -1)),
    (-3, (3, 1, -1)),
    (6, (-2, 1, -1)),
    (-6, (1, -1)),
)


def place(offset):
    if offset <= -16:
        offset += NZ
    if -7 <= offset <= 8:
        at = (offset + 7) // 2
    else:
        step = (offset - 9) // 2 if offset > 0 else (-offset - 8) // 2
        at = 8 + 4 * (step // 2) + step % 2 + (0 if offset > 0 else 2)
    return offset % 2 * 16 + at


assert sorted(place(o) for o in range(-15, 17)) == list(range(NZ))


def iota(shape, axis):
    return lax.broadcasted_iota(jnp.int32, shape, axis)


def dot(a, b):
    return jnp.dot(a, b, preferred_element_type=F32)


def dot_nt(a, b):
    return lax.dot_general(a, b, (((1,), (1,)), ((), ())), preferred_element_type=F32)


def kernel(
    feat_in,
    lists_in,
    w1s_in,
    w1n_in,
    w2s_in,
    w2n_in,
    rows_in_hbm,
    count_in_hbm,
    target_in_hbm,
    og_in,
    out_hbm,
    gs_hbm,
    gn_hbm,
    feat_ref,
    lists_ref,
    w1s_ref,
    w1n_ref,
    w2s_ref,
    w2n_ref,
    rows_ref,
    count_ref,
    target_ref,
    og_ref,
    out_ref,
    gs_ref,
    gn_ref,
    xs,
    xp,
    tiles,
    slots,
    relay_up,
    relay_down,
    w,
    w_own,
    w_relay,
    meta,
    gm_all,
    h_all,
    gh_own,
    gh_opp,
    gp,
    part,
    part_in,
    res,
    res_in,
    local_s,
    x_s,
    x_r,
    relay_s,
    relay_r,
    wz_s,
    wz_r,
    wr_r,
    wd_s,
    wd_r,
    meta_s,
    meta_r,
    gm_s,
    gm_r,
    h_s,
    h_r,
    gh_s,
    gh_r,
    hello,
    gp_s,
    gp_r,
    d2d_s,
    d2d_r,
):
    f = lax.axis_index("feat")
    d = lax.axis_index("dp")
    z = f // 2
    q = lax.rem(f, 2)
    partner = {"feat": 2 * z + 1 - q}
    sends = []

    def chip(offset):
        return {"feat": 2 * lax.rem(z + offset + NZ, NZ) + q}

    def row_peer(i):
        return lax.rem(d + i, NDP)

    def copy(src, dst, send, recv, device):
        return pltpu.make_async_remote_copy(
            src_ref=src, dst_ref=dst, send_sem=send, recv_sem=recv, device_id=device, device_id_type=MESH
        )

    def send(src, dst, send_sem, recv_sem, device):
        c = copy(src, dst, send_sem, recv_sem, device)
        c.start()
        sends.append(c)
        return c

    def arrived(dst, recv_sem):
        copy(dst, dst, d2d_s.at[0], recv_sem, partner).wait_recv()

    def to_row(src, dst, send_sem, recv_sem):
        @pl.loop(1, NDP)
        def _(i):
            copy(src, dst, send_sem.at[i], recv_sem.at[d], {"dp": row_peer(i)}).start()

    def from_row(buf, recv_sem):
        @pl.loop(1, NDP)
        def _(i):
            e = row_peer(i)
            arrived(buf.at[e], recv_sem.at[e])

    pairs = (
        (feat_in, feat_ref),
        (lists_in, lists_ref),
        (rows_in_hbm, rows_ref),
        (count_in_hbm, count_ref),
        (target_in_hbm, target_ref),
        (w1s_in, w1s_ref),
        (w1n_in, w1n_ref),
        (og_in, og_ref),
        (w2n_in, w2n_ref),
        (w2s_in, w2s_ref),
    )
    loads = [pltpu.make_async_copy(src, dst, local_s.at[n]) for n, (src, dst) in enumerate(pairs)]
    for c in loads[:2]:
        c.start()

    barrier = pltpu.get_barrier_semaphore()

    def signal(device):
        pl.semaphore_signal(barrier, inc=1, device_id=device, device_id_type=MESH)

    for offset in range(8, 0, -1):
        signal(chip(offset))
        signal(chip(-offset))
    signal(partner)

    @pl.loop(1, NDP)
    def _(i):
        signal({"dp": row_peer(i)})

    for c in loads[2:]:
        c.start()
    for c in loads[:2]:
        c.wait()

    chunks = [feat_ref[:, LANES * i : LANES * (i + 1)].astype(F32) for i in range(16)]

    @pl.loop(0, GROUPS)
    def _(c):
        lanes = pl.ds(pl.multiple_of(c * LANES, LANES), LANES)
        total = jnp.zeros((16, LANES), F32)
        for k in range(K1):
            index = jnp.broadcast_to(lists_ref[k, :, lanes], (16, LANES))
            low = lax.bitwise_and(index, 127)
            high = lax.shift_right_logical(index, 7)
            value = jnp.zeros((16, LANES), F32)
            for i in range(16):
                picked = jnp.take_along_axis(chunks[i], low, axis=1, mode="promise_in_bounds")
                value = jnp.where(high == i, picked, value)
            total += value
        xs[c, 0] = feat_ref[:, lanes]
        xs[c, 1] = (total / K1).astype(BF16)

    quarter = iota((16, LANES), 1) // 32

    @pl.loop(0, GROUPS)
    def _(c):
        far = lax.rem(c + 4, GROUPS)
        parts = [xs[c, 0], xs[c, 1], xs[far, 0], xs[far, 1]]
        parts = [p.astype(F32) for p in parts]
        for i in range(4):
            tile = jnp.zeros((16, LANES), F32)
            for k in range(4):
                shift = (32 * (k - i)) % LANES
                moved = pltpu.roll(parts[k], shift, 1) if shift else parts[k]
                tile = jnp.where(quarter == k, moved, tile)
            tiles[lax.rem(4 * c + i - z + NZ, NZ)] = tile.astype(BF16)

    slots[place(0)] = tiles[0]

    lane = iota((1, LANES), 1)
    slot = lax.rem(lane, 8)
    peer_rows = iota((NDP, LANES), 0) == iota((NDP, LANES), 1) // 8
    spread = peer_rows.astype(F32).astype(BF16)
    own_slot = iota((8, LANES), 0) == lax.rem(iota((8, LANES), 1), 8)

    for c in loads[2:7]:
        c.wait()

    def flat(ref):
        wide = dot(ref[...].astype(F32).astype(BF16), spread)
        return jnp.sum(jnp.where(own_slot, wide, 0.0), axis=0, keepdims=True)

    rows_own = flat(rows_ref)
    target_own = flat(target_ref)
    count_own = dot(count_ref[...].astype(F32).astype(BF16), spread)
    meta[d] = jnp.concatenate([rows_own, target_own, count_own, jnp.zeros((5, LANES), F32)], axis=0)

    piece = lax.rem(d, 8)
    w_lanes = pl.ds(pl.multiple_of(lax.rem(d, 4) * LANES, LANES), LANES)
    parity = d // 8
    own_tile = jnp.where(piece < 4, w1s_ref[:, w_lanes].astype(F32), w1n_ref[:, w_lanes].astype(F32)).astype(BF16)
    w_own[...] = own_tile

    @pl.when(parity == 0)
    def _():
        w[d, pl.ds(16 * place(0), 16), :] = own_tile

    def w_at(offset):
        return w.at[d, pl.ds(16 * (place(offset) % 16), 16), :]

    pl.semaphore_wait(barrier, 16 + 1 + NDP - 1)

    send(tiles.at[pl.ds(9, 8)], relay_up, relay_s.at[0], relay_r.at[0], chip(8))
    send(tiles.at[pl.ds(17, 7)], relay_down, relay_s.at[1], relay_r.at[1], chip(-8))

    w_direct, w_passed, w_near, w_far = [], [], [], []
    for p in (0, 1):
        up, down = (w_at(-8), w_at(8)) if p == 0 else (w_relay.at[0], w_relay.at[1])
        up_sem, down_sem = (
            (wz_r.at[place(-8) % 16], wz_r.at[place(8) % 16]) if p == 0 else (wr_r.at[0], wr_r.at[1])
        )
        near = [t for k in range(7, 0, -1) for t in (k, -k) if k % 2 == p]
        direct = [(8, up, up_sem), (-8, down, down_sem)]
        direct += [(t, w_at(-t), wz_r.at[place(-t) % 16]) for t in near]
        w_direct.append([copy(w_own, dst, wz_s.at[n], sem, chip(t)) for n, (t, dst, sem) in enumerate(direct)])
        passed = [(up, -8 - t, t) for t in range(8, 0, -1) if t % 2 == p]
        passed += [(down, 8 + t, -t) for t in range(7, 0, -1) if t % 2 == p]
        w_passed.append(
            [
                copy(src, w_at(offset), wz_s.at[10 + n], wz_r.at[place(offset) % 16], chip(t))
                for n, (src, offset, t) in enumerate(passed)
            ]
        )
        w_near.append(near)
        w_far.append([offset + (NZ if offset == -16 else 0) for _, offset, _ in passed])

    def by_parity(body):
        for p in (0, 1):
            pl.when(parity == p)(functools.partial(body, p))

    def start_weights(p):
        for c in w_direct[p]:
            c.start()

    def pass_weights(p):
        if p == 0:
            arrived(w_at(-8), wz_r.at[place(-8) % 16])
            arrived(w_at(8), wz_r.at[place(8) % 16])
        else:
            arrived(w_relay.at[0], wr_r.at[0])
            arrived(w_relay.at[1], wr_r.at[1])
        for c in w_passed[p]:
            c.start()
        for t in w_near[p]:
            arrived(w_at(-t), wz_r.at[place(-t) % 16])

    def far_weights(p, first):
        for offset in w_far[p]:
            if (place(offset) % 16 < 12) == first:
                arrived(w_at(offset), wz_r.at[place(offset) % 16])

    def sent_weights(p):
        for c in w_direct[p] + w_passed[p]:
            c.wait_send()

    by_parity(start_weights)

    for k in range(8, 0, -1):
        for t in (k, -k):
            send(tiles.at[t % NZ], slots.at[place(-t)], x_s.at[t + 8], x_r.at[place(-t)], chip(t))

    to_row(meta.at[d], meta.at[d], meta_s, meta_r)

    loads[7].wait()
    loads[8].wait()
    og = og_ref[...]
    raw_mean = dot_nt(og, w2n_ref[...])
    gm_all[d] = raw_mean.astype(BF16)
    to_row(gm_all.at[d], gm_all.at[d], gm_s, gm_r)
    pl.semaphore_signal(hello, inc=1, device_id=chip(8), device_id_type=MESH)
    send(xs, xp, d2d_s.at[0], d2d_r.at[0], partner)
    loads[9].wait()
    grad_self = dot_nt(og, w2s_ref[...])

    from_row(meta, meta_r)
    mine = iota((NDP, LANES), 1) // 8 == d
    same_slot = (lax.rem(iota((LANES, LANES), 0), 8) == lax.rem(iota((LANES, LANES), 1), 8)).astype(BF16)

    def from_peers(row):
        wide = dot(jnp.where(mine, meta[:, row, :], 0.0).astype(BF16), same_slot)
        return jnp.sum(jnp.where(peer_rows, wide, 0.0), axis=0, keepdims=True)

    rows_in = from_peers(0)
    target_in = from_peers(1)
    count_in = from_peers(2)
    slot_f = slot.astype(F32)
    base = (lane // 8 * 16).astype(F32)
    node = iota((16, LANES), 0).astype(F32)
    hits_in = jnp.where((target_own == node) & (slot_f < count_in), 1.0, 0.0)
    degree = jnp.sum(hits_in, axis=1, keepdims=True)

    hits_out = jnp.where((rows_own == node) & (slot_f < count_own), 1.0, 0.0)
    everyone = iota((NDP * 16, LANES), 0).astype(F32)
    table_in = jnp.where(everyone == base + rows_in, 1.0, 0.0).astype(BF16)
    table_out = jnp.where(everyone == base + target_in, 1.0, 0.0).astype(BF16)
    mix_in = dot_nt(hits_in.astype(BF16), table_in).astype(BF16)
    mix_out = dot_nt(hits_out.astype(BF16), table_out).astype(BF16)

    first_lane = (iota((NDP, LANES), 1) == 8 * iota((NDP, LANES), 0)).astype(F32).astype(BF16)
    count_to = dot_nt(first_lane, meta[:, 2, :].astype(BF16)).astype(BF16)
    live = lax.rem(iota((NDP, LANES), 1), 8).astype(F32) < dot(count_to, spread)
    aims = jnp.where(live, meta[:, 1, :], 31.0).astype(BF16)
    repeat = (iota((NDP * 16, NDP), 0) // 16 == iota((NDP * 16, NDP), 1)).astype(F32).astype(BF16)
    hits = dot(repeat, aims) == lax.rem(iota((NDP * 16, LANES), 0), 16).astype(F32)
    degrees = jnp.sum(jnp.where(hits, 1.0, 0.0), axis=1, keepdims=True)

    from_row(gm_all, gm_r)
    returned = gm_all[...].reshape(NDP * 16, 512).astype(F32) / (1.0 + degrees)
    back = jnp.dot(mix_out.astype(F32), returned, precision=lax.Precision.HIGHEST, preferred_element_type=F32)
    gh_own[...] = (grad_self + raw_mean / (1.0 + degree) + back).astype(BF16)
    pl.semaphore_wait(hello, 1)
    send(gh_own, gh_opp, gh_s.at[0], gh_r.at[0], chip(16))

    arrived(relay_up, relay_r.at[0])
    for t in range(8, 0, -1):
        send(relay_up.at[t - 1], slots.at[place(-8 - t)], x_s.at[16 + t], x_r.at[place(-8 - t)], chip(t))
    arrived(relay_down, relay_r.at[1])
    for t in range(7, 0, -1):
        send(relay_down.at[7 - t], slots.at[place(8 + t)], x_s.at[24 + t], x_r.at[place(8 + t)], chip(-t))

    by_parity(pass_weights)
    spans = (pl.ds(0, 128), pl.ds(128, 64), pl.ds(192, 64))

    def weights_to_row(n):
        to_row(w.at[d, spans[n]], w.at[d, spans[n]], wd_s.at[n], wd_r.at[n])

    def weights_from_row(n):
        @pl.loop(1, NDP)
        def _(i):
            e = row_peer(i)
            arrived(w.at[e, spans[n]], wd_r.at[n, e])

    weights_to_row(0)

    arrived(xp, d2d_r.at[0])
    node_in = iota((1024, 512), 0)
    node_at = iota((1024, 512), 1)
    block_at = node_at // 16
    chip_at = lax.rem(z - 7 + NZ + block_at // 2 + 16 * lax.rem(block_at, 2), NZ)
    pick = jnp.where(node_in == 32 * chip_at + 16 * q + lax.rem(node_at, 16), 1.0, 0.0).astype(BF16)
    wide_rows = jnp.concatenate(
        [
            jnp.concatenate([buf[c, kind] for c in range(GROUPS)], axis=1)
            for buf in (xs, xp)
            for kind in (0, 1)
        ],
        axis=0,
    )
    x_cols = dot(wide_rows, pick).astype(BF16)

    by_parity(functools.partial(far_weights, first=True))
    weights_to_row(1)
    by_parity(functools.partial(far_weights, first=False))
    weights_to_row(2)

    for offset in range(-15, 17):
        if offset:
            arrived(slots.at[place(offset)], x_r.at[place(offset)])
    turned = [
        jnp.transpose(slots[16 * half : 16 * half + 16].reshape(256, LANES).astype(F32)).astype(BF16)
        for half in (0, 1)
    ]

    def rows_of(half, kind):
        t = turned[half]
        return jnp.concatenate([t[32 * kind : 32 * kind + 32], t[64 + 32 * kind : 96 + 32 * kind]], axis=0)

    x_rows = [[rows_of(half, kind) for kind in (0, 1)] for half in (0, 1)]

    def products(block, k):
        total = jnp.zeros((64, LANES), F32)
        for half in (0, 1):
            for kind in (0, 1):
                total += dot(x_rows[half][kind][:, k], w[half * 8 + kind * 4 + block, k])
        return total

    weights_from_row(0)
    first_sums = [products(block, slice(0, 128)) for block in range(4)]
    weights_from_row(1)
    weights_from_row(2)
    for block in range(4):
        total = first_sums[block] + products(block, slice(128, 256))
        lanes = slice(LANES * block, LANES * (block + 1))
        for core in (0, 1):
            part[core, 0:16, lanes] = total[16 * core : 16 * core + 16]
            part[core, 16:32, lanes] = total[32 + 16 * core : 48 + 16 * core]

    send(part.at[1 - q], part_in, d2d_s.at[1], d2d_r.at[1], partner)
    arrived(part_in, d2d_r.at[1])
    preact = part[q] + part_in[...]
    hidden = jnp.maximum(preact[0:16], 0.0).astype(BF16)
    arrived(gh_opp, gh_r.at[0])
    gp[7, 0] = jnp.where(preact[0:16] > 0, gh_own[...].astype(F32), 0.0).astype(BF16)
    gp[7, 1] = jnp.where(preact[16:32] > 0, gh_opp[...].astype(F32), 0.0).astype(BF16)
    h_all[d] = hidden

    def pass_on(offset, targets):
        for target in targets:
            there = offset - target + 7
            send(gp.at[offset + 7], gp.at[there], gp_s.at[there], gp_r.at[there], chip(target))

    pass_on(*WINDOW_PLAN[0])
    to_row(h_all.at[d], h_all.at[d], h_s, h_r)
    for offset, targets in WINDOW_PLAN[1:]:
        arrived(gp.at[offset + 7], gp_r.at[offset + 7])
        pass_on(offset, targets)

    from_row(h_all, h_r)
    stores = [
        pltpu.make_async_copy(src, dst, local_s.at[10 + n])
        for n, (src, dst) in enumerate(((out_ref, out_hbm), (gs_ref, gs_hbm), (gn_ref, gn_hbm)))
    ]
    neigh_sum = dot(mix_in, h_all[...].reshape(NDP * 16, 512))
    mean_two = ((hidden.astype(F32) + neigh_sum) / (1.0 + degree)).astype(BF16)
    out_ref[...] = (dot(hidden, w2s_ref[...]) + dot(mean_two, w2n_ref[...])).astype(BF16)
    stores[0].start()

    for offset in range(-7, 9):
        if offset not in [o for o, _ in WINDOW_PLAN]:
            arrived(gp.at[offset + 7], gp_r.at[offset + 7])

    res[...] = dot(x_cols, gp[...].reshape(512, 512))
    send(res.at[32:64], res_in, d2d_s.at[2], d2d_r.at[2], partner)
    arrived(res_in, d2d_r.at[2])
    gs_ref[...] = res[0:16] + res_in[0:16]
    gn_ref[...] = res[16:32] + res_in[16:32]

    stores[1].start()
    stores[2].start()

    for c in sends:
        c.wait_send()

    by_parity(sent_weights)

    @pl.loop(1, NDP)
    def _(i):
        to = {"dp": row_peer(i)}
        copy(meta.at[d], meta.at[d], meta_s.at[i], meta_r.at[d], to).wait_send()
        copy(gm_all.at[d], gm_all.at[d], gm_s.at[i], gm_r.at[d], to).wait_send()
        copy(h_all.at[d], h_all.at[d], h_s.at[i], h_r.at[d], to).wait_send()
        for n in range(3):
            copy(w.at[d, spans[n]], w.at[d, spans[n]], wd_s.at[n, i], wd_r.at[n, d], to).wait_send()

    for c in stores:
        c.wait()


def on_device(
    features,
    neigh_lists,
    w1_self,
    w1_neigh,
    w2_self,
    w2_neigh,
    send_rows,
    send_count,
    recv_target,
    out_grad,
):
    dma = pltpu.SemaphoreType.DMA
    hbm = pl.BlockSpec(memory_space=pl.ANY)
    layer_out, grad_self, grad_neigh = pl.pallas_call(
        kernel,
        out_shape=(
            jax.ShapeDtypeStruct((16, 512), BF16),
            jax.ShapeDtypeStruct((16, 512), F32),
            jax.ShapeDtypeStruct((16, 512), F32),
        ),
        in_specs=[hbm] * 10,
        out_specs=(hbm, hbm, hbm),
        scratch_shapes=[
            pltpu.VMEM((16, 2048), BF16),
            pltpu.VMEM((K1, 1, 1024), jnp.int32),
            pltpu.VMEM((16, 512), BF16),
            pltpu.VMEM((16, 512), BF16),
            pltpu.VMEM((512, 512), BF16),
            pltpu.VMEM((512, 512), BF16),
            pltpu.VMEM((8, 16), jnp.int32),
            pltpu.VMEM((1, 16), jnp.int32),
            pltpu.VMEM((8, 16), jnp.int32),
            pltpu.VMEM((16, 512), BF16),
            pltpu.VMEM((16, 512), BF16),
            pltpu.VMEM((16, 512), F32),
            pltpu.VMEM((16, 512), F32),
            pltpu.VMEM((GROUPS, 2, 16, LANES), BF16),
            pltpu.VMEM((GROUPS, 2, 16, LANES), BF16),
            pltpu.VMEM((NZ, 16, LANES), BF16),
            pltpu.VMEM((NZ, 16, LANES), BF16),
            pltpu.VMEM((8, 16, LANES), BF16),
            pltpu.VMEM((7, 16, LANES), BF16),
            pltpu.VMEM((NDP, 256, LANES), BF16),
            pltpu.VMEM((16, LANES), BF16),
            pltpu.VMEM((2, 16, LANES), BF16),
            pltpu.VMEM((NDP, 8, LANES), F32),
            pltpu.VMEM((NDP, 16, 512), BF16),
            pltpu.VMEM((NDP, 16, 512), BF16),
            pltpu.VMEM((16, 512), BF16),
            pltpu.VMEM((16, 512), BF16),
            pltpu.VMEM((16, 2, 16, 512), BF16),
            pltpu.VMEM((2, 32, 512), F32),
            pltpu.VMEM((32, 512), F32),
            pltpu.VMEM((64, 512), F32),
            pltpu.VMEM((32, 512), F32),
            dma((13,)),
            dma((NZ,)),
            dma((NZ,)),
            dma((2,)),
            dma((2,)),
            dma((18,)),
            dma((16,)),
            dma((2,)),
            dma((3, NDP)),
            dma((3, NDP)),
            dma((NDP,)),
            dma((NDP,)),
            dma((NDP,)),
            dma((NDP,)),
            dma((NDP,)),
            dma((NDP,)),
            dma((1,)),
            dma((1,)),
            pltpu.SemaphoreType.REGULAR,
            dma((16,)),
            dma((16,)),
            dma((3,)),
            dma((3,)),
        ],
        compiler_params=pltpu.CompilerParams(
            collective_id=0, has_side_effects=True, vmem_limit_bytes=64 * 1024 * 1024
        ),
    )(
        features[0],
        jnp.transpose(neigh_lists, (1, 0, 2)),
        w1_self,
        w1_neigh,
        w2_self,
        w2_neigh,
        jnp.transpose(send_rows[0, 0]),
        send_count[0],
        jnp.transpose(recv_target[0, 0]),
        out_grad[0, 0],
    )
    return layer_out[None, None], grad_self[None], grad_neigh[None]


def solution(mesh):
    in_specs = (
        P("dp", "feat", None),
        P("dp", None, None),
        P("feat", None),
        P("feat", None),
        P(),
        P(),
        P("dp", "feat", None, None),
        P("dp", "feat", None),
        P("dp", "feat", None, None),
        P("dp", "feat", None, None),
    )
    out_specs = (P("dp", "feat", None, None), P("dp", "feat", None), P("dp", "feat", None))
    return jax.shard_map(
        on_device, mesh=mesh, in_specs=in_specs, out_specs=out_specs, check_vma=False
    )
```
